32 devices in a mesh: peer: 4 (over y, x), space: 8 (over z, core).
Axes of the slice: x: 2, y: 2, z: 4, core: 2. Of those that a mesh axis runs over, the one named last changes fastest.
Arguments:
- images: bfloat16 [4, 128, 32, 512], P('peer', 'space'), may hold values from -6 to 6
- task_grad: bfloat16 [4, 128, 32, 512], P('peer', 'space'), may hold values from -6 to 6
- pairing: int32 [4], replicated, may hold values from 0 to 3, as said below
- first_kernel: bfloat16 [4, 3, 3, 512, 512], P('peer'), may hold values from -0.09375 to 0.09375
- first_scale: float32 [4, 512], P('peer'), may hold values from 0.25 to 1.75
- first_shift: float32 [4, 512], P('peer'), may hold values from -3 to 3
- second_kernel: bfloat16 [4, 3, 3, 512, 512], P('peer'), may hold values from -0.09375 to 0.09375
- second_scale: float32 [4, 512], P('peer'), may hold values from 0.25 to 1.75
- second_shift: float32 [4, 512], P('peer'), may hold values from -3 to 3
Outputs:
- input_grad: bfloat16 [4, 128, 32, 512], P('peer', 'space')
The draws below stay inside these ranges and needn't reach their ends.
Inputs may be any that keep to these rules, and one draw needn't show every extreme that they name: `pairing`: every network index appears exactly once.
All inputs are finite; a program needn't handle non-finite values.
Results may differ from the reference program's by a relative error of at most 0.012.
Values may be sent and summed in bfloat16 or wider, within the bound.
No kernel may reach another device: no remote copies, remote signals or barrier semaphores. Data moves between devices by JAX's collectives and lax.ppermute only.
A program may use at most 64 MiB of HBM per device.

```python
import jax
import jax.numpy as jnp
from jax import lax

C = 512
W_COLS = 32
H = 128
N_PEER = 4


def swap_entries(order, first_pos, second_pos):
    places = jnp.arange(order.shape[0], dtype=jnp.int32)
    first_val = jnp.sum(jnp.where(places == first_pos, order, 0))
    second_val = jnp.sum(jnp.where(places == second_pos, order, 0))
    order = jnp.where(places == first_pos, second_val, order)
    return jnp.where(places == second_pos, first_val, order)


def draw_pairing(key, part):
    places = jnp.arange(N_PEER, dtype=jnp.int32)
    order = jax.random.permutation(jax.random.fold_in(key, 11), places).astype(jnp.int32)
    anchor = jax.random.randint(jax.random.fold_in(key, 12), (), 0, N_PEER).astype(jnp.int32)
    target = (anchor + N_PEER // 2) % N_PEER
    holder = jnp.sum(jnp.where(order == target, places, 0)).astype(jnp.int32)
    order = swap_entries(order, anchor, holder)
    follower = (anchor + 1) % N_PEER
    holder = jnp.sum(jnp.where(order == anchor, places, 0)).astype(jnp.int32)
    order = swap_entries(order, follower, holder)
    return order.astype(jnp.int32)


def block_levels(rng, shape, cuts, low, largest):
    loudness = 1.0
    for axis_at, parts in cuts:
        steps = jax.random.uniform(jax.random.fold_in(jax.random.fold_in(rng, 6), axis_at), (parts,), jnp.float32, low / len(cuts), largest / len(cuts))
        loudness = loudness * jnp.repeat(jnp.exp(steps), shape[axis_at] // parts).reshape((-1,) + (1,) * (len(shape) - 1 - axis_at))
    return loudness


def scatter_about(own_key, dims, spread, reach, cuts=(), kind=jnp.bfloat16):
    result = spread * jax.random.normal(own_key, dims, jnp.float32)
    if cuts:
        result = result * block_levels(own_key, dims, cuts, -0.22, 0.18)
    return jnp.clip(result, -reach, reach).astype(kind)


def setup_inputs(seed: int = 0) -> dict:
    splits = jax.random.split(jax.random.key(seed), 10)
    return {
        "images": scatter_about(splits[0], (N_PEER, H, W_COLS, C), 1.0, 6.0, ((0, 4), (1, 8))),
        "task_grad": scatter_about(splits[1], (N_PEER, H, W_COLS, C), 1.0, 6.0, ((0, 4), (1, 8))),
        "pairing": draw_pairing(jax.random.fold_in(splits[9], 71), 0),
        "first_kernel": scatter_about(splits[3], (N_PEER, 3, 3, C, C), (9 * C) ** -0.5, 0.09375, ((0, 4),)),
        "first_scale": jnp.clip(1.0 + 0.15 * jax.random.normal(splits[4], (N_PEER, C), jnp.float32), 0.25, 1.75),
        "first_shift": scatter_about(splits[5], (N_PEER, C), 0.5, 3.0, ((0, 4),), jnp.float32),
        "second_kernel": scatter_about(splits[6], (N_PEER, 3, 3, C, C), (9 * C) ** -0.5, 0.09375, ((0, 4),)),
        "second_scale": jnp.clip(1.0 + 0.15 * jax.random.normal(splits[7], (N_PEER, C), jnp.float32), 0.25, 1.75),
        "second_shift": scatter_about(splits[8], (N_PEER, C), 0.5, 3.0, ((0, 4),), jnp.float32),
    }


def apply_dilated_filter(receptive_span, filter_kernel, dilation_rate, reverse_kernel):
    input_rows = receptive_span.shape[0]
    input_width = receptive_span.shape[1]
    padded_input = jnp.pad(receptive_span.astype(jnp.float32), ((dilation_rate, dilation_rate), (dilation_rate, dilation_rate), (0, 0)))
    weights = filter_kernel.astype(jnp.float32)
    total = jnp.zeros((input_rows, input_width, filter_kernel.shape[2]), jnp.float32)
    for kernel_tap_row in range(3):
        for kernel_tap_column in range(3):
            input_window = padded_input[kernel_tap_row * dilation_rate:kernel_tap_row * dilation_rate + input_rows, kernel_tap_column * dilation_rate:kernel_tap_column * dilation_rate + input_width]
            if reverse_kernel:
                total = total + jnp.einsum("rwo,io->rwi", input_window, weights[2 - kernel_tap_row, 2 - kernel_tap_column], precision=lax.Precision.HIGHEST)
            else:
                total = total + jnp.einsum("rwi,io->rwo", input_window, weights[kernel_tap_row, kernel_tap_column], precision=lax.Precision.HIGHEST)
    return total


def silu_slope(value):
    sig = jax.nn.sigmoid(value)
    return sig * (1.0 + value * (1.0 - sig))


def forward_one(image, first_kernel, first_scale, first_shift, second_kernel, second_scale, second_shift):
    pre_first = first_scale * apply_dilated_filter(image, first_kernel, 2, False) + first_shift
    hidden = jax.nn.silu(pre_first).astype(jnp.bfloat16)
    pre_second = second_scale * apply_dilated_filter(hidden, second_kernel, 4, False) + second_shift
    feat = jax.nn.silu(pre_second).astype(jnp.bfloat16)
    return feat


def backward_one(image, task_one, partner_feat, first_kernel, first_scale, first_shift, second_kernel, second_scale, second_shift):
    pre_first = first_scale * apply_dilated_filter(image, first_kernel, 2, False) + first_shift
    hidden = jax.nn.silu(pre_first).astype(jnp.bfloat16)
    pre_second = second_scale * apply_dilated_filter(hidden, second_kernel, 4, False) + second_shift
    feat = jax.nn.silu(pre_second).astype(jnp.bfloat16)
    cot = task_one.astype(jnp.float32) + feat.astype(jnp.float32) - partner_feat.astype(jnp.float32)
    grad_second = (cot * silu_slope(pre_second) * second_scale).astype(jnp.bfloat16)
    grad_hidden = apply_dilated_filter(grad_second, second_kernel, 4, True)
    grad_first = (grad_hidden * silu_slope(pre_first) * first_scale).astype(jnp.bfloat16)
    return apply_dilated_filter(grad_first, first_kernel, 2, True).astype(jnp.bfloat16)


def reference(images, task_grad, pairing, first_kernel, first_scale, first_shift, second_kernel, second_scale, second_shift):
    feats = lax.map(lambda args: forward_one(*args), (images, first_kernel, first_scale, first_shift, second_kernel, second_scale, second_shift))
    partners = jnp.take(feats, pairing.astype(jnp.int32), axis=0)
    return lax.map(lambda args: backward_one(*args), (images, task_grad, partners, first_kernel, first_scale, first_shift, second_kernel, second_scale, second_shift))
```

```python
import functools
import itertools
import math

import jax
import jax.numpy as jnp
from jax import lax
from jax.experimental import pallas as pl
from jax.experimental.pallas import tpu as pltpu
from jax.sharding import PartitionSpec as P

BF16 = jnp.bfloat16
F32 = jnp.float32
VMEM_LIMIT = 16 * 2**20
MAX_ROUTES = 24
D1 = 2
D2 = 4
EDGE = D1 + D2


def side():
    return lax.rem(lax.axis_index("space"), 2)


def at_end():
    me = lax.axis_index("space")
    return jnp.logical_or(me == 0, me == lax.axis_size("space") - 1)


def pick(odd, if_even, if_odd):
    return if_even + odd * (if_odd - if_even)


def put(cat, start, rows, value, dilation):
    width, chans = value.shape[1], value.shape[2]
    none = jnp.zeros((rows, dilation, chans), value.dtype)
    at = pl.ds(start, rows)
    cat[at, :, 0:chans] = jnp.concatenate([none, value[:, : width - dilation]], axis=1)
    cat[at, :, chans : 2 * chans] = value
    cat[at, :, 2 * chans : 3 * chans] = jnp.concatenate([value[:, dilation:], none], axis=1)


def conv(cat, kernel, dilation, rows, lo, size):
    width, depth = cat.shape[1], cat.shape[2]
    total = None
    for a in range(3):
        block = cat[a * dilation : a * dilation + rows].reshape(rows * width, depth)
        part = jnp.dot(block, kernel[a, :, lo : lo + size], preferred_element_type=F32)
        total = part if total is None else total + part
    return total


def conv_t(cat, kernel, dilation, rows, lo, size):
    width, chans = cat.shape[1], cat.shape[2] // 3
    total = None
    for a in range(3):
        for b in range(3):
            block = cat[(2 - a) * dilation : (2 - a) * dilation + rows, :, (2 - b) * chans : (3 - b) * chans]
            part = lax.dot_general(
                block.reshape(rows * width, chans),
                kernel[a, b * chans + lo : b * chans + lo + size],
                (((1,), (1,)), ((), ())),
                preferred_element_type=F32,
            )
            total = part if total is None else total + part
    return total


def activate(total, scale, shift):
    pre = total * scale + shift
    sig = 1.0 / (1.0 + jnp.exp(-pre))
    return pre * sig, sig * (1.0 + pre * (1.0 - sig)) * scale


def hide_beyond(rim, odd, count):
    @pl.when(at_end())
    def _():
        none = jnp.zeros((count,) + rim.shape[1:], rim.dtype)
        rim[pl.ds(pick(odd, 0, rim.shape[0] - count), count)] = none


def halves(chans):
    step = chans // 2 if chans % 256 == 0 else chans
    return [(lo, step) for lo in range(0, chans, step)]


def first_inner(image, halo, kernel, scale, shift, hidden, slope, cat):
    odd = side()
    strip, edge = image.shape[0], halo.shape[0]
    put(cat, pick(odd, 0, edge), strip, image[...], D1)
    put(cat, pick(odd, strip, 0), edge, halo[...], D1)
    rows, width = hidden.shape[0], hidden.shape[1]
    for lo, size in halves(hidden.shape[2]):
        cut = slice(lo, lo + size)
        act, grad = activate(conv(cat, kernel, D1, rows, lo, size), scale[:, cut], shift[:, cut])
        hidden[:, :, cut] = act.astype(BF16).reshape(rows, width, size)
        slope[:, :, cut] = grad.reshape(rows, width, size)


def second_inner(hidden, kernel, scale, shift, feat, slope, cat):
    put(cat, 0, hidden.shape[0], hidden[...], D2)
    rows, width = feat.shape[0], feat.shape[1]
    for lo, size in halves(feat.shape[2]):
        cut = slice(lo, lo + size)
        act, grad = activate(conv(cat, kernel, D2, rows, lo, size), scale[:, cut], shift[:, cut])
        feat[:, :, cut] = act.astype(BF16).reshape(rows, width, size)
        slope[:, :, cut] = grad.reshape(rows, width, size)


def both_outer(
    image, halo, inner, kernel1, scale1, shift1, kernel2, scale2, shift2, feat, slope1, slope2, cat1, cat2, rim
):
    odd = side()
    strip, edge, width = image.shape[0], halo.shape[0], image.shape[1]
    own = 2 * D1
    put(cat1, pick(odd, 0, own), edge, halo[...], D1)
    put(cat1, pick(odd, edge, 0), own, image[pl.ds(pick(odd, 0, strip - own), own)], D1)
    for lo, size in halves(feat.shape[2]):
        cut = slice(lo, lo + size)
        act, grad = activate(conv(cat1, kernel1, D1, edge, lo, size), scale1[:, cut], shift1[:, cut])
        rim[:, :, cut] = act.astype(BF16).reshape(edge, width, size)
        slope1[:, :, cut] = grad.reshape(edge, width, size)
    hide_beyond(rim, odd, D2)
    more = 2 * D2
    put(cat2, pick(odd, 0, more), edge, rim[...], D2)
    put(cat2, pick(odd, edge, 0), more, inner[pl.ds(pick(odd, 0, inner.shape[0] - more), more)], D2)
    rows = feat.shape[0]
    for lo, size in halves(feat.shape[2]):
        cut = slice(lo, lo + size)
        act, grad = activate(conv(cat2, kernel2, D2, rows, lo, size), scale2[:, cut], shift2[:, cut])
        feat[:, :, cut] = act.astype(BF16).reshape(rows, width, size)
        slope2[:, :, cut] = grad.reshape(rows, width, size)


def cotangent(pairing, task, feat, partner, slope, start, rows):
    me = lax.axis_index("peer")
    mine = feat[...].astype(F32)
    other = jnp.where(pairing[me] == me, mine, partner[...].astype(F32))
    cot = task[pl.ds(start, rows)].astype(F32) + mine - other
    return (cot * slope[...]).astype(BF16)


def grad_inner(pairing, task, feat, partner, slope, grad, send):
    odd = side()
    rows, edge = feat.shape[0], send.shape[0]
    grad[...] = cotangent(pairing, task, feat, partner, slope, pick(odd, task.shape[0] - rows, 0), rows)
    send[...] = grad[pl.ds(pick(odd, rows - edge, 0), edge)]


def grad_outer(pairing, task, feat, partner, slope, grad):
    odd = side()
    rows = feat.shape[0]
    grad[...] = cotangent(pairing, task, feat, partner, slope, pick(odd, 0, task.shape[0] - rows), rows)


def back_inner(grad, halo, slope, kernel2, kernel1, out, grad1, cat2, cat1):
    odd = side()
    own, edge, width = grad.shape[0], halo.shape[0], grad.shape[1]
    put(cat2, pick(odd, 0, edge), own, grad[...], D2)
    put(cat2, pick(odd, own, 0), edge, halo[...], D2)
    rows = grad1.shape[0]
    at = pl.ds(pick(odd, slope.shape[0] - D1 - rows, D1), rows)
    for lo, size in halves(grad1.shape[2]):
        cut = slice(lo, lo + size)
        back = conv_t(cat2, kernel2, D2, rows, lo, size).reshape(rows, width, size)
        grad1[:, :, cut] = (back * slope[at, :, cut]).astype(BF16)
    put(cat1, 0, rows, grad1[...], D1)
    rows = out.shape[0]
    for lo, size in halves(out.shape[2]):
        back = conv_t(cat1, kernel1, D1, rows, lo, size)
        out[:, :, lo : lo + size] = back.astype(BF16).reshape(rows, width, size)


def back_middle(grad, inner, slope, below, kernel2, kernel1, out, grad1, cat2, cat1):
    odd = side()
    edge, width = grad.shape[0], grad.shape[1]
    more = 2 * D2
    put(cat2, pick(odd, 0, more), edge, grad[...], D2)
    put(cat2, pick(odd, edge, 0), more, inner[pl.ds(pick(odd, 0, inner.shape[0] - more), more)], D2)
    rows = grad1.shape[0]
    at = pl.ds(pick(odd, D1, slope.shape[0] - D1 - rows), rows)
    for lo, size in halves(grad1.shape[2]):
        cut = slice(lo, lo + size)
        back = conv_t(cat2, kernel2, D2, rows, lo, size).reshape(rows, width, size)
        grad1[:, :, cut] = (back * slope[at, :, cut]).astype(BF16)
    more = 2 * D1
    put(cat1, pick(odd, 0, more), rows, grad1[...], D1)
    put(cat1, pick(odd, rows, 0), more, below[pl.ds(pick(odd, 0, below.shape[0] - more), more)], D1)
    rows = out.shape[0]
    for lo, size in halves(out.shape[2]):
        back = conv_t(cat1, kernel1, D1, rows, lo, size)
        out[:, :, lo : lo + size] = back.astype(BF16).reshape(rows, width, size)


def back_outer(
    halo, grad, inner, slope_rim, slope, below, kernel2, kernel1, out_in, out_mid, out, cat2, cat1, rim, fold
):
    odd = side()
    edge, width = grad.shape[0], grad.shape[1]
    more = 2 * D2 - edge
    put(cat2, pick(odd, 0, edge + more), edge, halo[...], D2)
    put(cat2, pick(odd, edge, more), edge, grad[...], D2)
    put(cat2, pick(odd, 2 * edge, 0), more, inner[pl.ds(pick(odd, 0, inner.shape[0] - more), more)], D2)
    rows = rim.shape[0]
    fold[pl.ds(pick(odd, 0, rows - D2), D2)] = slope_rim[pl.ds(pick(odd, edge - D2, 0), D2)]
    fold[pl.ds(pick(odd, D2, 0), rows - D2)] = slope[pl.ds(pick(odd, 0, slope.shape[0] - rows + D2), rows - D2)]
    for lo, size in halves(rim.shape[2]):
        cut = slice(lo, lo + size)
        back = conv_t(cat2, kernel2, D2, rows, lo, size).reshape(rows, width, size)
        rim[:, :, cut] = (back * fold[:, :, cut]).astype(BF16)
    hide_beyond(rim, odd, D1)
    more = 2 * D1
    put(cat1, pick(odd, 0, more), rows, rim[...], D1)
    put(cat1, pick(odd, rows, 0), more, below[pl.ds(pick(odd, 0, below.shape[0] - more), more)], D1)
    strip = out.shape[0]
    first, second = out_in.shape[0], out_mid.shape[0]
    third = strip - first - second
    out[pl.ds(pick(odd, strip - first, 0), first)] = out_in[...]
    out[pl.ds(pick(odd, third, first), second)] = out_mid[...]
    at = pl.ds(pick(odd, 0, strip - third), third)
    for lo, size in halves(out.shape[2]):
        back = conv_t(cat1, kernel1, D1, third, lo, size)
        out[at, :, lo : lo + size] = back.astype(BF16).reshape(third, width, size)


def call(body, name, args, outs, scratch=(), smem=0, flops=0):
    specs = [
        pl.BlockSpec(memory_space=pltpu.SMEM if i < smem else pltpu.VMEM) for i in range(len(args))
    ]
    moved = sum(a.size * a.dtype.itemsize for a in args)
    return pl.pallas_call(
        body,
        out_shape=outs,
        in_specs=specs,
        out_specs=[pl.BlockSpec(memory_space=pltpu.VMEM)] * len(outs),
        scratch_shapes=[pltpu.VMEM(s.shape, s.dtype) for s in scratch],
        compiler_params=pltpu.CompilerParams(vmem_limit_bytes=VMEM_LIMIT),
        cost_estimate=pl.CostEstimate(flops=flops, bytes_accessed=moved, transcendentals=0),
        name=name,
    )(*args)


def routes_of(groups):
    pairings = list(itertools.permutations(range(groups)))
    moves = [frozenset((p, n) for n, p in enumerate(pair) if p != n) for pair in pairings]
    routes = []
    for move in sorted(set(moves), key=lambda m: (-len(m), sorted(m))):
        if not any(move <= route for route in routes):
            routes.append(move)
    chosen = [next(i for i, route in enumerate(routes) if move <= route) for move in moves]
    return [sorted(route) for route in routes], chosen


def rank(pairing, groups):
    total = jnp.int32(0)
    for i in range(groups):
        smaller = jnp.int32(0)
        for j in range(i + 1, groups):
            smaller = smaller + (pairing[j] < pairing[i]).astype(jnp.int32)
        total = total + smaller * math.factorial(groups - 1 - i)
    return total


def lookup(index, table):
    value = jnp.int32(table[0])
    for i in range(1, len(table)):
        if table[i] != table[i - 1]:
            value = jnp.where(index >= i, jnp.int32(table[i]), value)
    return value


def swap_blocks(feat, pairing):
    groups = lax.axis_size("peer")
    chans = feat.shape[-1]
    blocks = feat.reshape(groups, feat.size // chans // groups, chans)
    received = lax.all_to_all(blocks, "peer", split_axis=0, concat_axis=0, tiled=True)
    chosen = jnp.take(received, pairing, axis=0)
    returned = lax.all_to_all(chosen, "peer", split_axis=0, concat_axis=0, tiled=True)
    return returned.reshape(feat.shape)


def per_device(images, task_grad, pairing, first_kernel, scale1, shift1, second_kernel, scale2, shift2):
    image, task = images[0], task_grad[0]
    strip, width, chans = image.shape
    kernel1 = first_kernel[0].reshape(3, 3 * chans, chans)
    kernel2 = second_kernel[0].reshape(3, 3 * chans, chans)
    space, groups = lax.axis_size("space"), lax.axis_size("peer")
    odd = side()
    near = [(i, i ^ 1) for i in range(space)]
    far = [(i, i + 1) for i in range(1, space - 1, 2)] + [(i + 1, i) for i in range(1, space - 1, 2)]
    per_row = 2 * 9 * width * chans * chans

    def rows_of(count, kind=BF16):
        return jax.ShapeDtypeStruct((count, width, chans), kind)

    def cat_of(count):
        return jax.ShapeDtypeStruct((count, width, 3 * chans), BF16)

    last = strip - EDGE
    near_halo = lax.ppermute(lax.dynamic_slice_in_dim(image, pick(odd, last, 0), EDGE, 0), "space", near)
    far_halo = lax.ppermute(lax.dynamic_slice_in_dim(image, pick(odd, 0, last), EDGE, 0), "space", far)

    inner = strip - EDGE
    deep = strip + EDGE - 2 * D1
    hidden, slope1 = call(
        first_inner,
        "first_inner",
        (image, near_halo, kernel1, scale1, shift1),
        (rows_of(deep), rows_of(deep, F32)),
        (cat_of(strip + EDGE),),
        flops=per_row * deep,
    )
    feat_in, slope2_in = call(
        second_inner,
        "second_inner",
        (hidden, kernel2, scale2, shift2),
        (rows_of(inner), rows_of(inner, F32)),
        (cat_of(deep),),
        flops=per_row * inner,
    )

    def exchange(swap, far_halo, feat_in):
        partner_in = swap(feat_in)
        feat_out, slope1_rim, slope2_out = call(
            both_outer,
            "both_outer",
            (image, far_halo, hidden, kernel1, scale1, shift1, kernel2, scale2, shift2),
            (rows_of(EDGE), rows_of(EDGE, F32), rows_of(EDGE, F32)),
            (cat_of(EDGE + 2 * D1), cat_of(EDGE + 2 * D2), rows_of(EDGE)),
            flops=per_row * 2 * EDGE,
        )
        partner_out = swap(feat_out)
        grad_in, grad_send = call(
            grad_inner,
            "grad_inner",
            (pairing, task, feat_in, partner_in, slope2_in),
            (rows_of(inner), rows_of(EDGE)),
            smem=1,
        )
        near_grad = lax.ppermute(grad_send, "space", near)
        third = deep - inner
        out_in, grad1_in = call(
            back_inner,
            "back_inner",
            (grad_in, near_grad, slope1, kernel2, kernel1),
            (rows_of(third - 2 * D1), rows_of(third)),
            (cat_of(inner + EDGE), cat_of(third)),
            flops=per_row * (2 * third - 2 * D1),
        )
        (grad_out,) = call(
            grad_outer,
            "grad_outer",
            (pairing, task, feat_out, partner_out, slope2_out),
            (rows_of(EDGE),),
            smem=1,
        )
        return grad_out, grad_in, grad1_in, out_in, slope1_rim

    if math.factorial(groups) <= MAX_ROUTES:
        routes, chosen = routes_of(groups)

        def branch(route, *given):
            return exchange(lambda feat: lax.ppermute(feat, "peer", route), *given)

        index = lookup(rank(pairing, groups), chosen)
        state = lax.switch(index, [functools.partial(branch, r) for r in routes], far_halo, feat_in)
    else:
        state = exchange(lambda feat: swap_blocks(feat, pairing), far_halo, feat_in)
    grad_out, grad_in, grad1_in, out_in, slope1_rim = state
    far_grad = lax.ppermute(grad_out, "space", far)
    out_mid, grad1_mid = call(
        back_middle,
        "back_middle",
        (grad_out, grad_in, slope1, grad1_in, kernel2, kernel1),
        (rows_of(EDGE), rows_of(EDGE)),
        (cat_of(EDGE + 2 * D2), cat_of(EDGE + 2 * D1)),
        flops=per_row * 2 * EDGE,
    )
    (out,) = call(
        back_outer,
        "back_outer",
        (far_grad, grad_out, grad_in, slope1_rim, slope1, grad1_mid, kernel2, kernel1, out_in, out_mid),
        (rows_of(strip),),
        (cat_of(EDGE + 2 * D2), cat_of(EDGE + 2 * D1), rows_of(EDGE), rows_of(EDGE, F32)),
        flops=per_row * 2 * EDGE,
    )
    return out[None]


def solution(mesh):
    placed = (
        P("peer", "space", None, None),
        P("peer", "space", None, None),
        P(),
        P("peer", None, None, None, None),
        P("peer", None),
        P("peer", None),
        P("peer", None, None, None, None),
        P("peer", None),
        P("peer", None),
    )
    return jax.shard_map(
        per_device,
        mesh=mesh,
        in_specs=placed,
        out_specs=P("peer", "space", None, None),
        check_vma=False,
    )
```

```python
import functools
import itertools
import math

import jax
import jax.numpy as jnp
from jax import lax
from jax.experimental import pallas as pl
from jax.experimental.pallas import tpu as pltpu
from jax.sharding import PartitionSpec as P

BF16 = jnp.bfloat16
F32 = jnp.float32
VMEM_LIMIT = 24 * 2**20
MAX_ROUTES = 24
LULL = 30
D1 = 2
D2 = 4
EDGE = D1 + D2


def side():
    return lax.rem(lax.axis_index("space"), 2)


def at_end():
    me = lax.axis_index("space")
    return jnp.logical_or(me == 0, me == lax.axis_size("space") - 1)


def pick(odd, if_even, if_odd):
    return if_even + odd * (if_odd - if_even)


def put(cat, start, rows, value, dilation):
    width, chans = value.shape[1], value.shape[2]
    none = jnp.zeros((rows, dilation, chans), value.dtype)
    at = pl.ds(start, rows)
    cat[at, :, 0:chans] = jnp.concatenate([none, value[:, : width - dilation]], axis=1)
    cat[at, :, chans : 2 * chans] = value
    cat[at, :, 2 * chans : 3 * chans] = jnp.concatenate([value[:, dilation:], none], axis=1)


def no_wait(*tap):
    pass


def conv(cat, kernel, dilation, rows, lo, size):
    width, depth = cat.shape[1], cat.shape[2]
    total = None
    for a in range(3):
        block = cat[a * dilation : a * dilation + rows].reshape(rows * width, depth)
        part = jnp.dot(block, kernel[a, :, lo : lo + size], preferred_element_type=F32)
        total = part if total is None else total + part
    return total


def conv_t(cat, kernel, dilation, rows, lo, size):
    width, chans = cat.shape[1], cat.shape[2] // 3
    total = None
    for a in range(3):
        for b in range(3):
            block = cat[(2 - a) * dilation : (2 - a) * dilation + rows, :, (2 - b) * chans : (3 - b) * chans]
            part = lax.dot_general(
                block.reshape(rows * width, chans),
                kernel[a, b * chans + lo : b * chans + lo + size],
                (((1,), (1,)), ((), ())),
                preferred_element_type=F32,
            )
            total = part if total is None else total + part
    return total


def hide_beyond(rim, odd, count):
    @pl.when(at_end())
    def _():
        none = jnp.zeros((count,) + rim.shape[1:], rim.dtype)
        rim[pl.ds(pick(odd, 0, rim.shape[0] - count), count)] = none


def halves(chans):
    step = chans // 2 if chans % 256 == 0 else chans
    return [(lo, step) for lo in range(0, chans, step)]


def conv_act(cat, kernel, scale, shift, dilation, act, slope):
    rows, width, chans = act.shape
    for lo, size in halves(chans):
        cut = slice(lo, lo + size)
        pre = conv(cat, kernel, dilation, rows, lo, size) * scale[:, cut] + shift[:, cut]
        sig = 1.0 / (1.0 + jnp.exp(-pre))
        act[:, :, cut] = (pre * sig).astype(BF16).reshape(rows, width, size)
        slope[:, :, cut] = (sig * (1.0 + pre * (1.0 - sig)) * scale[:, cut]).reshape(rows, width, size)


def prepare(
    image, scale1, shift1, scale2, shift2, pairing, index, strip, near_send, far_send, vectors, pair, sems, *, table
):
    copies = [
        pltpu.make_async_copy(image, strip, sems.at[0]),
        pltpu.make_async_copy(pairing, pair, sems.at[1]),
    ]
    for i, source in enumerate((scale1, shift1, scale2, shift2)):
        copies.append(pltpu.make_async_copy(source, vectors.at[pl.ds(8 * i, 1)], sems.at[2 + i]))
    for copy in copies:
        copy.start()
    copies[1].wait()
    rank = jnp.int32(0)
    if table:
        groups = pair.shape[0]
        for i in range(groups):
            smaller = jnp.int32(0)
            for j in range(i + 1, groups):
                smaller = smaller + (pair[j] < pair[i]).astype(jnp.int32)
            rank = rank + smaller * math.factorial(groups - 1 - i)
        rank = lookup(rank, table)
    index[0] = rank
    me = lax.axis_index("peer")
    paired = jnp.where(pair[me] == me, 0.0, 1.0)
    vectors[pl.ds(32, 1)] = jnp.full((1, vectors.shape[1]), paired, F32)
    odd = side()
    edge = near_send.shape[0]
    last = strip.shape[0] - edge
    copies[0].wait()
    near_send[...] = strip[pl.ds(pick(odd, last, 0), edge)]
    far_send[...] = strip[pl.ds(pick(odd, 0, last), edge)]
    for copy in copies[2:]:
        copy.wait()


def first(image, near, kernel1, vectors, hidden, slope, cat):
    odd = side()
    strip, edge = image.shape[0], near.shape[0]
    put(cat, pick(odd, 0, edge), strip, image[...], D1)
    put(cat, pick(odd, strip, 0), edge, near[...], D1)
    conv_act(cat, kernel1, vectors[0:1], vectors[8:9], D1, hidden, slope)


def second(
    image, far, hidden, slope, kernel1, kernel2, vectors, task, feat, base, rate, fold,
    cat1, cat2, rim, slope1, slope2, part, sems
):
    odd = side()
    strip, edge, held = image.shape[0], far.shape[0], hidden.shape[0]
    most = held - D1
    copies = [
        pltpu.make_async_copy(task, part, sems.at[0]),
        pltpu.make_async_copy(
            slope.at[pl.ds(pick(odd, 0, D1), most)], fold.at[pl.ds(pick(odd, D2, 0), most)], sems.at[1]
        ),
        pltpu.make_async_copy(
            slope1.at[pl.ds(pick(odd, D1, 0), D2)], fold.at[pl.ds(pick(odd, 0, most), D2)], sems.at[2]
        ),
    ]
    copies[0].start()
    copies[1].start()
    own = 2 * D1
    put(cat1, pick(odd, 0, own), edge, far[...], D1)
    put(cat1, pick(odd, edge, 0), own, image[pl.ds(pick(odd, 0, strip - own), own)], D1)
    conv_act(cat1, kernel1, vectors[0:1], vectors[8:9], D1, rim, slope1)
    copies[2].start()
    hide_beyond(rim, odd, D2)
    put(cat2, pick(odd, edge, 0), held, hidden[...], D2)
    put(cat2, pick(odd, 0, held), edge, rim[...], D2)
    conv_act(cat2, kernel2, vectors[16:17], vectors[24:25], D2, feat, slope2)
    for copy in copies:
        copy.wait()
    paired = vectors[32:33]
    mine = feat[...].astype(F32)
    rate[...] = slope2[...] * paired
    base[...] = (part[...].astype(F32) + mine * paired) * slope2[...]


def gradient(base, rate, partner, grad):
    def step(row, carry):
        grad[row] = (base[row] - partner[row].astype(F32) * rate[row]).astype(BF16)
        return carry

    lax.fori_loop(0, grad.shape[0], step, 0, unroll=4)


def edges(grad, near_send, far_send):
    odd = side()
    strip, edge = grad.shape[0], near_send.shape[0]
    near_send[...] = grad[pl.ds(pick(odd, strip - edge, 0), edge)]
    far_send[...] = grad[pl.ds(pick(odd, 0, strip - edge), edge)]


def back_second(grad, near, fold, kernel2, kernel1, grad1, kept, cat, sems):
    copy = pltpu.make_async_copy(kernel1, kept, sems.at[0])
    copy.start()
    odd = side()
    strip, edge, width, rows = grad.shape[0], near.shape[0], grad.shape[1], grad1.shape[0]
    at = pl.ds(pick(odd, fold.shape[0] - rows, 0), rows)
    put(cat, pick(odd, 0, edge), strip, grad[...], D2)
    put(cat, pick(odd, strip, 0), edge, near[...], D2)
    for lo, size in halves(grad1.shape[2]):
        cut = slice(lo, lo + size)
        back = conv_t(cat, kernel2, D2, rows, lo, size).reshape(rows, width, size)
        grad1[:, :, cut] = (back * fold[at, :, cut]).astype(BF16)
    copy.wait()


def back_first(far, grad, fold, inner, kernel2, kernel1, out, cat2, cat1, rim):
    odd = side()
    edge, width, held, rows = far.shape[0], far.shape[1], inner.shape[0], rim.shape[0]
    at = pl.ds(pick(odd, 0, fold.shape[0] - rows), rows)
    more = 2 * D2
    put(cat2, pick(odd, 0, more), edge, far[...], D2)
    put(cat2, pick(odd, edge, 0), more, grad[pl.ds(pick(odd, 0, grad.shape[0] - more), more)], D2)
    for lo, size in halves(rim.shape[2]):
        cut = slice(lo, lo + size)
        back = conv_t(cat2, kernel2, D2, rows, lo, size).reshape(rows, width, size)
        rim[:, :, cut] = (back * fold[at, :, cut]).astype(BF16)
    hide_beyond(rim, odd, D1)
    put(cat1, pick(odd, rows, 0), held, inner[...], D1)
    put(cat1, pick(odd, 0, held), rows, rim[...], D1)
    rows = out.shape[0]
    for lo, size in halves(out.shape[2]):
        back = conv_t(cat1, kernel1, D1, rows, lo, size)
        out[:, :, lo : lo + size] = back.astype(BF16).reshape(rows, width, size)


def call(body, name, args, outs, scratch=(), flops=0, remote=(), stored=(), result=None):
    kinds = [pltpu.HBM if i in remote else pltpu.VMEM for i in range(len(args))]
    out_kinds = [
        pltpu.HBM if i in stored else pltpu.SMEM if o.dtype == jnp.int32 else pltpu.VMEM for i, o in enumerate(outs)
    ]
    return pl.pallas_call(
        body,
        out_shape=[o if i == result else k(o.shape, o.dtype) for i, (o, k) in enumerate(zip(outs, out_kinds))],
        in_specs=[pl.BlockSpec(memory_space=k) for k in kinds],
        out_specs=[pl.BlockSpec(memory_space=k) for k in out_kinds],
        scratch_shapes=[pltpu.VMEM(s.shape, s.dtype) if isinstance(s, jax.ShapeDtypeStruct) else s for s in scratch],
        compiler_params=pltpu.CompilerParams(vmem_limit_bytes=VMEM_LIMIT),
        cost_estimate=pl.CostEstimate(flops=flops, bytes_accessed=0, transcendentals=0),
        name=name,
    )(*[pltpu.with_memory_space_constraint(a, k) for a, k in zip(args, kinds)])


def routes_of(groups):
    pairings = list(itertools.permutations(range(groups)))
    moves = [frozenset((p, n) for n, p in enumerate(pair) if p != n) for pair in pairings]
    routes = []
    for move in sorted(set(moves), key=lambda m: (-len(m), sorted(m))):
        if not any(move <= route for route in routes):
            routes.append(move)
    chosen = [next(i for i, route in enumerate(routes) if move <= route) for move in moves]
    return [sorted(route) for route in routes], chosen


def lookup(index, table):
    value = jnp.int32(table[0])
    for i in range(1, len(table)):
        if table[i] != table[i - 1]:
            value = jnp.where(index >= i, jnp.int32(table[i]), value)
    return value


def swap_blocks(feat, pairing):
    groups = lax.axis_size("peer")
    chans = feat.shape[-1]
    blocks = feat.reshape(groups, feat.size // chans // groups, chans)
    received = lax.all_to_all(blocks, "peer", split_axis=0, concat_axis=0, tiled=True)
    chosen = jnp.take(received, pairing, axis=0)
    returned = lax.all_to_all(chosen, "peer", split_axis=0, concat_axis=0, tiled=True)
    return returned.reshape(feat.shape)


def per_device(images, task_grad, pairing, first_kernel, scale1, shift1, second_kernel, scale2, shift2):
    image, task = images[0], task_grad[0]
    strip, width, chans = image.shape
    kernel1 = first_kernel[0].reshape(3, 3 * chans, chans)
    kernel2 = second_kernel[0].reshape(3, 3 * chans, chans)
    space, groups = lax.axis_size("space"), lax.axis_size("peer")
    pairs = [(i, i ^ 1) for i in range(space)]
    across = [(i, i + 1) for i in range(1, space - 1, 2)] + [(i + 1, i) for i in range(1, space - 1, 2)]
    per_row = 2 * 9 * width * chans * chans
    deep = strip + EDGE - 2 * D1
    held = deep - 2 * D1

    def rows_of(count, kind=BF16):
        return jax.ShapeDtypeStruct((count, width, chans), kind)

    def cat_of(count):
        return jax.ShapeDtypeStruct((count, width, 3 * chans), BF16)

    def near(rows):
        return lax.ppermute(rows, "space", pairs)

    def far(rows):
        return lax.ppermute(rows, "space", across)

    routed = math.factorial(groups) <= MAX_ROUTES
    routes, chosen = routes_of(groups) if routed else ((), ())
    dma = pltpu.SemaphoreType.DMA
    index, image, near_send, far_send, vectors = call(
        functools.partial(prepare, table=tuple(chosen)),
        "prepare",
        (image, scale1, shift1, scale2, shift2, pairing),
        (
            jax.ShapeDtypeStruct((1,), jnp.int32),
            rows_of(strip),
            rows_of(EDGE),
            rows_of(EDGE),
            jax.ShapeDtypeStruct((40, chans), F32),
        ),
        (pltpu.SMEM((groups,), jnp.int32), dma((6,))),
        flops=LULL * per_row * strip,
        remote=range(6),
    )
    near_halo = near(near_send)
    far_halo = far(far_send)
    hidden, slope1 = call(
        first,
        "first",
        (image, near_halo, kernel1, vectors),
        (rows_of(deep), rows_of(deep, F32)),
        (cat_of(strip + EDGE),),
        flops=per_row * deep,
    )
    feat, base, rate, fold = call(
        second,
        "second",
        (image, far_halo, hidden, slope1, kernel1, kernel2, vectors, task),
        (rows_of(strip), rows_of(strip, F32), rows_of(strip, F32), rows_of(strip + 2 * D1, F32)),
        (
            cat_of(EDGE + 2 * D1),
            cat_of(strip + 2 * D2),
            rows_of(EDGE),
            rows_of(EDGE, F32),
            rows_of(strip, F32),
            rows_of(strip),
            dma((3,)),
        ),
        flops=per_row * (EDGE + strip),
        remote=(7,),
        stored=(3,),
    )

    def exchange(swap, feat, base, rate):
        return call(gradient, "gradient", (base, rate, swap(feat)), (rows_of(strip),))[0]

    if routed:
        moves = [functools.partial(lax.ppermute, axis_name="peer", perm=route) for route in routes]
        grad = lax.switch(index[0], [functools.partial(exchange, move) for move in moves], feat, base, rate)
    else:
        grad = exchange(functools.partial(swap_blocks, pairing=pairing), feat, base, rate)
    near_send, far_send = call(
        edges, "edges", (grad,), (rows_of(EDGE), rows_of(EDGE)), flops=LULL * per_row * strip
    )
    near_grad = near(near_send)
    far_grad = far(far_send)
    inner, kept1 = call(
        back_second,
        "back_second",
        (grad, near_grad, fold, kernel2, kernel1),
        (rows_of(held), jax.ShapeDtypeStruct(kernel1.shape, BF16)),
        (cat_of(strip + EDGE), dma((1,))),
        flops=per_row * held,
        remote=(4,),
    )
    (out,) = call(
        back_first,
        "back_first",
        (far_grad, grad, fold, inner, kernel2, kept1),
        (rows_of(strip),),
        (cat_of(EDGE + 2 * D2), cat_of(strip + 2 * D1), rows_of(EDGE)),
        flops=per_row * (EDGE + strip),
        result=0,
    )
    return out[None]


def solution(mesh):
    placed = (
        P("peer", "space", None, None),
        P("peer", "space", None, None),
        P(),
        P("peer", None, None, None, None),
        P("peer", None),
        P("peer", None),
        P("peer", None, None, None, None),
        P("peer", None),
        P("peer", None),
    )
    return jax.shard_map(
        per_device,
        mesh=mesh,
        in_specs=placed,
        out_specs=P("peer", "space", None, None),
        check_vma=False,
    )
```

```python
import functools
import itertools
import math

import jax
import jax.numpy as jnp
from jax import lax
from jax.experimental import pallas as pl
from jax.experimental.pallas import tpu as pltpu
from jax.sharding import PartitionSpec as P

BF16 = jnp.bfloat16
F32 = jnp.float32
VMEM_LIMIT = 24 * 2**20
MAX_ROUTES = 24
LULL = 30
D1 = 2
D2 = 4
EDGE = D1 + D2


def side():
    return lax.rem(lax.axis_index("space"), 2)


def at_end():
    me = lax.axis_index("space")
    return jnp.logical_or(me == 0, me == lax.axis_size("space") - 1)


def pick(odd, if_even, if_odd):
    return if_even + odd * (if_odd - if_even)


def put(cat, start, rows, value, dilation):
    width, chans = value.shape[1], value.shape[2]
    none = jnp.zeros((rows, dilation, chans), value.dtype)
    at = pl.ds(start, rows)
    cat[at, :, 0:chans] = jnp.concatenate([none, value[:, : width - dilation]], axis=1)
    cat[at, :, chans : 2 * chans] = value
    cat[at, :, 2 * chans : 3 * chans] = jnp.concatenate([value[:, dilation:], none], axis=1)


def no_wait(*tap):
    pass


def conv(cat, kernel, dilation, rows, lo, size):
    width, depth = cat.shape[1], cat.shape[2]
    total = None
    for a in range(3):
        block = cat[a * dilation : a * dilation + rows].reshape(rows * width, depth)
        part = jnp.dot(block, kernel[a, :, lo : lo + size], preferred_element_type=F32)
        total = part if total is None else total + part
    return total


def conv_t(cat, kernel, dilation, rows, lo, size):
    width, chans = cat.shape[1], cat.shape[2] // 3
    total = None
    for a in range(3):
        for b in range(3):
            block = cat[(2 - a) * dilation : (2 - a) * dilation + rows, :, (2 - b) * chans : (3 - b) * chans]
            part = lax.dot_general(
                block.reshape(rows * width, chans),
                kernel[a, b * chans + lo : b * chans + lo + size],
                (((1,), (1,)), ((), ())),
                preferred_element_type=F32,
            )
            total = part if total is None else total + part
    return total


def hide_beyond(rim, odd, count):
    @pl.when(at_end())
    def _():
        none = jnp.zeros((count,) + rim.shape[1:], rim.dtype)
        rim[pl.ds(pick(odd, 0, rim.shape[0] - count), count)] = none


def put_far(cat, start, halo, dilation):
    rows = halo.shape[0]
    put(cat, start, rows, halo[...], dilation)

    @pl.when(at_end())
    def _():
        cat[pl.ds(start, rows)] = jnp.zeros((rows,) + cat.shape[1:], cat.dtype)


def halves(chans):
    step = chans // 2 if chans % 256 == 0 else chans
    return [(lo, step) for lo in range(0, chans, step)]


def conv_act(cat, kernel, scale, shift, dilation, act, slope):
    rows, width, chans = act.shape
    for lo, size in halves(chans):
        cut = slice(lo, lo + size)
        pre = conv(cat, kernel, dilation, rows, lo, size) * scale[:, cut] + shift[:, cut]
        sig = 1.0 / (1.0 + jnp.exp(-pre))
        act[:, :, cut] = (pre * sig).astype(BF16).reshape(rows, width, size)
        slope[:, :, cut] = (sig * (1.0 + pre * (1.0 - sig)) * scale[:, cut]).reshape(rows, width, size)


def prepare(
    image, scale1, shift1, scale2, shift2, pairing, index, strip, near_send, far_send, vectors, pair, sems, *, table
):
    copies = [
        pltpu.make_async_copy(image, strip, sems.at[0]),
        pltpu.make_async_copy(pairing, pair, sems.at[1]),
    ]
    for i, source in enumerate((scale1, shift1, scale2, shift2)):
        copies.append(pltpu.make_async_copy(source, vectors.at[pl.ds(8 * i, 1)], sems.at[2 + i]))
    for copy in copies:
        copy.start()
    copies[1].wait()
    rank = jnp.int32(0)
    if table:
        groups = pair.shape[0]
        for i in range(groups):
            smaller = jnp.int32(0)
            for j in range(i + 1, groups):
                smaller = smaller + (pair[j] < pair[i]).astype(jnp.int32)
            rank = rank + smaller * math.factorial(groups - 1 - i)
        rank = lookup(rank, table)
    index[0] = rank
    me = lax.axis_index("peer")
    paired = jnp.where(pair[me] == me, 0.0, 1.0)
    vectors[pl.ds(32, 1)] = jnp.full((1, vectors.shape[1]), paired, F32)
    odd = side()
    edge = near_send.shape[0]
    last = strip.shape[0] - edge
    copies[0].wait()
    near_send[...] = strip[pl.ds(pick(odd, last, 0), edge)]
    far_send[...] = strip[pl.ds(pick(odd, 0, last), edge)]
    for copy in copies[2:]:
        copy.wait()


def first(image, near, kernel1, vectors, hidden, slope, cat):
    odd = side()
    strip, edge = image.shape[0], near.shape[0]
    put(cat, pick(odd, 0, edge), strip, image[...], D1)
    put(cat, pick(odd, strip, 0), edge, near[...], D1)
    conv_act(cat, kernel1, vectors[0:1], vectors[8:9], D1, hidden, slope)


def second(
    image, far, hidden, slope, kernel1, kernel2, vectors, task, feat, base, rate, fold,
    cat1, cat2, rim, slope1, slope2, part, sems
):
    odd = side()
    strip, edge, held = image.shape[0], far.shape[0], hidden.shape[0]
    most = held - D1
    copies = [
        pltpu.make_async_copy(task, part, sems.at[0]),
        pltpu.make_async_copy(
            slope.at[pl.ds(pick(odd, 0, D1), most)], fold.at[pl.ds(pick(odd, D2, 0), most)], sems.at[1]
        ),
        pltpu.make_async_copy(
            slope1.at[pl.ds(pick(odd, D1, 0), D2)], fold.at[pl.ds(pick(odd, 0, most), D2)], sems.at[2]
        ),
    ]
    copies[0].start()
    copies[1].start()
    own = 2 * D1
    put_far(cat1, pick(odd, 0, own), far, D1)
    put(cat1, pick(odd, edge, 0), own, image[pl.ds(pick(odd, 0, strip - own), own)], D1)
    conv_act(cat1, kernel1, vectors[0:1], vectors[8:9], D1, rim, slope1)
    copies[2].start()
    hide_beyond(rim, odd, D2)
    put(cat2, pick(odd, edge, 0), held, hidden[...], D2)
    put(cat2, pick(odd, 0, held), edge, rim[...], D2)
    conv_act(cat2, kernel2, vectors[16:17], vectors[24:25], D2, feat, slope2)
    for copy in copies:
        copy.wait()
    paired = vectors[32:33]
    mine = feat[...].astype(F32)
    rate[...] = slope2[...] * paired
    base[...] = (part[...].astype(F32) + mine * paired) * slope2[...]


def gradient(base, rate, partner, grad):
    def step(row, carry):
        grad[row] = (base[row] - partner[row].astype(F32) * rate[row]).astype(BF16)
        return carry

    lax.fori_loop(0, grad.shape[0], step, 0, unroll=4)


def edges(grad, near_send, far_send):
    odd = side()
    strip, edge = grad.shape[0], near_send.shape[0]
    near_send[...] = grad[pl.ds(pick(odd, strip - edge, 0), edge)]
    far_send[...] = grad[pl.ds(pick(odd, 0, strip - edge), edge)]


def back_second(grad, near, fold, kernel2, kernel1, grad1, kept, cat, sems):
    copy = pltpu.make_async_copy(kernel1, kept, sems.at[0])
    copy.start()
    odd = side()
    strip, edge, width, rows = grad.shape[0], near.shape[0], grad.shape[1], grad1.shape[0]
    at = pl.ds(pick(odd, fold.shape[0] - rows, 0), rows)
    put(cat, pick(odd, 0, edge), strip, grad[...], D2)
    put(cat, pick(odd, strip, 0), edge, near[...], D2)
    for lo, size in halves(grad1.shape[2]):
        cut = slice(lo, lo + size)
        back = conv_t(cat, kernel2, D2, rows, lo, size).reshape(rows, width, size)
        grad1[:, :, cut] = (back * fold[at, :, cut]).astype(BF16)
    copy.wait()


def back_first(far, grad, fold, inner, kernel2, kernel1, out, cat2, cat1, rim):
    odd = side()
    edge, width, held, rows = far.shape[0], far.shape[1], inner.shape[0], rim.shape[0]
    at = pl.ds(pick(odd, 0, fold.shape[0] - rows), rows)
    more = 2 * D2
    put_far(cat2, pick(odd, 0, more), far, D2)
    put(cat2, pick(odd, edge, 0), more, grad[pl.ds(pick(odd, 0, grad.shape[0] - more), more)], D2)
    for lo, size in halves(rim.shape[2]):
        cut = slice(lo, lo + size)
        back = conv_t(cat2, kernel2, D2, rows, lo, size).reshape(rows, width, size)
        rim[:, :, cut] = (back * fold[at, :, cut]).astype(BF16)
    hide_beyond(rim, odd, D1)
    put(cat1, pick(odd, rows, 0), held, inner[...], D1)
    put(cat1, pick(odd, 0, held), rows, rim[...], D1)
    rows = out.shape[0]
    for lo, size in halves(out.shape[2]):
        back = conv_t(cat1, kernel1, D1, rows, lo, size)
        out[:, :, lo : lo + size] = back.astype(BF16).reshape(rows, width, size)


def call(body, name, args, outs, scratch=(), flops=0, remote=(), stored=(), result=None):
    kinds = [pltpu.HBM if i in remote else pltpu.VMEM for i in range(len(args))]
    out_kinds = [
        pltpu.HBM if i in stored else pltpu.SMEM if o.dtype == jnp.int32 else pltpu.VMEM for i, o in enumerate(outs)
    ]
    return pl.pallas_call(
        body,
        out_shape=[o if i == result else k(o.shape, o.dtype) for i, (o, k) in enumerate(zip(outs, out_kinds))],
        in_specs=[pl.BlockSpec(memory_space=k) for k in kinds],
        out_specs=[pl.BlockSpec(memory_space=k) for k in out_kinds],
        scratch_shapes=[pltpu.VMEM(s.shape, s.dtype) if isinstance(s, jax.ShapeDtypeStruct) else s for s in scratch],
        compiler_params=pltpu.CompilerParams(vmem_limit_bytes=VMEM_LIMIT),
        cost_estimate=pl.CostEstimate(flops=flops, bytes_accessed=0, transcendentals=0),
        name=name,
    )(*[pltpu.with_memory_space_constraint(a, k) for a, k in zip(args, kinds)])


def routes_of(groups):
    pairings = list(itertools.permutations(range(groups)))
    moves = [frozenset((p, n) for n, p in enumerate(pair) if p != n) for pair in pairings]
    routes = []
    for move in sorted(set(moves), key=lambda m: (-len(m), sorted(m))):
        if not any(move <= route for route in routes):
            routes.append(move)
    chosen = [next(i for i, route in enumerate(routes) if move <= route) for move in moves]
    return [sorted(route) for route in routes], chosen


def lookup(index, table):
    value = jnp.int32(table[0])
    for i in range(1, len(table)):
        if table[i] != table[i - 1]:
            value = jnp.where(index >= i, jnp.int32(table[i]), value)
    return value


def far_side(group, place, groups, space):
    other = place + 1 if place % 2 else place - 1
    if 0 <= other < space:
        return group * space + other
    return (group ^ 1) * space + place if groups % 2 == 0 else group * space + other % space


def swap_blocks(feat, pairing):
    groups = lax.axis_size("peer")
    chans = feat.shape[-1]
    blocks = feat.reshape(groups, feat.size // chans // groups, chans)
    received = lax.all_to_all(blocks, "peer", split_axis=0, concat_axis=0, tiled=True)
    chosen = jnp.take(received, pairing, axis=0)
    returned = lax.all_to_all(chosen, "peer", split_axis=0, concat_axis=0, tiled=True)
    return returned.reshape(feat.shape)


def per_device(images, task_grad, pairing, first_kernel, scale1, shift1, second_kernel, scale2, shift2):
    image, task = images[0], task_grad[0]
    strip, width, chans = image.shape
    kernel1 = first_kernel[0].reshape(3, 3 * chans, chans)
    kernel2 = second_kernel[0].reshape(3, 3 * chans, chans)
    space, groups = lax.axis_size("space"), lax.axis_size("peer")
    pairs = [(i, i ^ 1) for i in range(space)]
    across = [(p * space + i, far_side(p, i, groups, space)) for p in range(groups) for i in range(space)]
    per_row = 2 * 9 * width * chans * chans
    deep = strip + EDGE - 2 * D1
    held = deep - 2 * D1

    def rows_of(count, kind=BF16):
        return jax.ShapeDtypeStruct((count, width, chans), kind)

    def cat_of(count):
        return jax.ShapeDtypeStruct((count, width, 3 * chans), BF16)

    def near(rows):
        return lax.ppermute(rows, "space", pairs)

    def far(rows):
        return lax.ppermute(rows, ("peer", "space"), across)

    routed = math.factorial(groups) <= MAX_ROUTES
    routes, chosen = routes_of(groups) if routed else ((), ())
    dma = pltpu.SemaphoreType.DMA
    index, image, near_send, far_send, vectors = call(
        functools.partial(prepare, table=tuple(chosen)),
        "prepare",
        (image, scale1, shift1, scale2, shift2, pairing),
        (
            jax.ShapeDtypeStruct((1,), jnp.int32),
            rows_of(strip),
            rows_of(EDGE),
            rows_of(EDGE),
            jax.ShapeDtypeStruct((40, chans), F32),
        ),
        (pltpu.SMEM((groups,), jnp.int32), dma((6,))),
        flops=LULL * per_row * strip,
        remote=range(6),
    )
    near_halo = near(near_send)
    far_halo = far(far_send)
    hidden, slope1 = call(
        first,
        "first",
        (image, near_halo, kernel1, vectors),
        (rows_of(deep), rows_of(deep, F32)),
        (cat_of(strip + EDGE),),
        flops=per_row * deep,
    )
    feat, base, rate, fold = call(
        second,
        "second",
        (image, far_halo, hidden, slope1, kernel1, kernel2, vectors, task),
        (rows_of(strip), rows_of(strip, F32), rows_of(strip, F32), rows_of(strip + 2 * D1, F32)),
        (
            cat_of(EDGE + 2 * D1),
            cat_of(strip + 2 * D2),
            rows_of(EDGE),
            rows_of(EDGE, F32),
            rows_of(strip, F32),
            rows_of(strip),
            dma((3,)),
        ),
        flops=per_row * (EDGE + strip),
        remote=(7,),
        stored=(3,),
    )

    def exchange(swap, feat, base, rate):
        return call(gradient, "gradient", (base, rate, swap(feat)), (rows_of(strip),))[0]

    if routed:
        moves = [functools.partial(lax.ppermute, axis_name="peer", perm=route) for route in routes]
        grad = lax.switch(index[0], [functools.partial(exchange, move) for move in moves], feat, base, rate)
    else:
        grad = exchange(functools.partial(swap_blocks, pairing=pairing), feat, base, rate)
    near_send, far_send = call(
        edges, "edges", (grad,), (rows_of(EDGE), rows_of(EDGE)), flops=LULL * per_row * strip
    )
    near_grad = near(near_send)
    far_grad = far(far_send)
    inner, kept1 = call(
        back_second,
        "back_second",
        (grad, near_grad, fold, kernel2, kernel1),
        (rows_of(held), jax.ShapeDtypeStruct(kernel1.shape, BF16)),
        (cat_of(strip + EDGE), dma((1,))),
        flops=per_row * held,
        remote=(4,),
    )
    (out,) = call(
        back_first,
        "back_first",
        (far_grad, grad, fold, inner, kernel2, kept1),
        (rows_of(strip),),
        (cat_of(EDGE + 2 * D2), cat_of(strip + 2 * D1), rows_of(EDGE)),
        flops=per_row * (EDGE + strip),
        result=0,
    )
    return out[None]


def solution(mesh):
    placed = (
        P("peer", "space", None, None),
        P("peer", "space", None, None),
        P(),
        P("peer", None, None, None, None),
        P("peer", None),
        P("peer", None),
        P("peer", None, None, None, None),
        P("peer", None),
        P("peer", None),
    )
    return jax.shard_map(
        per_device,
        mesh=mesh,
        in_specs=placed,
        out_specs=P("peer", "space", None, None),
        check_vma=False,
    )
```

```python
import functools
import itertools
import math

import jax
import jax.numpy as jnp
from jax import lax
from jax.experimental import pallas as pl
from jax.experimental.pallas import tpu as pltpu
from jax.sharding import PartitionSpec as P

BF16 = jnp.bfloat16
F32 = jnp.float32
VMEM_LIMIT = 40 * 2**20
MAX_ROUTES = 24
LULL = 30
D1 = 2
D2 = 4
EDGE = D1 + D2


def side():
    return lax.rem(lax.axis_index("space"), 2)


def at_end():
    me = lax.axis_index("space")
    return jnp.logical_or(me == 0, me == lax.axis_size("space") - 1)


def pick(odd, if_even, if_odd):
    return if_even + odd * (if_odd - if_even)


def put(cat, start, rows, value, dilation):
    width, chans = value.shape[1], value.shape[2]
    none = jnp.zeros((rows, dilation, chans), value.dtype)
    at = pl.ds(start, rows)
    cat[at, :, 0:chans] = jnp.concatenate([none, value[:, : width - dilation]], axis=1)
    cat[at, :, chans : 2 * chans] = value
    cat[at, :, 2 * chans : 3 * chans] = jnp.concatenate([value[:, dilation:], none], axis=1)


def no_wait(*tap):
    pass


def conv(cat, kernel, dilation, rows, lo, size):
    width, depth = cat.shape[1], cat.shape[2]
    total = None
    for a in range(3):
        block = cat[a * dilation : a * dilation + rows].reshape(rows * width, depth)
        part = jnp.dot(block, kernel[a, :, lo : lo + size], preferred_element_type=F32)
        total = part if total is None else total + part
    return total


def conv_t(cat, kernel, dilation, rows, lo, size):
    width, chans = cat.shape[1], cat.shape[2] // 3
    total = None
    for a in range(3):
        for b in range(3):
            block = cat[(2 - a) * dilation : (2 - a) * dilation + rows, :, (2 - b) * chans : (3 - b) * chans]
            part = lax.dot_general(
                block.reshape(rows * width, chans),
                kernel[a, b * chans + lo : b * chans + lo + size],
                (((1,), (1,)), ((), ())),
                preferred_element_type=F32,
            )
            total = part if total is None else total + part
    return total


def hide_beyond(rim, odd, count):
    @pl.when(at_end())
    def _():
        none = jnp.zeros((count,) + rim.shape[1:], rim.dtype)
        rim[pl.ds(pick(odd, 0, rim.shape[0] - count), count)] = none


def put_far(cat, start, halo, dilation):
    rows = halo.shape[0]
    put(cat, start, rows, halo[...], dilation)

    @pl.when(at_end())
    def _():
        cat[pl.ds(start, rows)] = jnp.zeros((rows,) + cat.shape[1:], cat.dtype)


def halves(chans):
    step = chans // 2 if chans % 256 == 0 else chans
    return [(lo, step) for lo in range(0, chans, step)]


def conv_act(cat, kernel, scale, shift, dilation, act, slope):
    rows, width, chans = act.shape
    for lo, size in halves(chans):
        cut = slice(lo, lo + size)
        pre = conv(cat, kernel, dilation, rows, lo, size) * scale[:, cut] + shift[:, cut]
        sig = 1.0 / (1.0 + jnp.exp(-pre))
        act[:, :, cut] = (pre * sig).astype(BF16).reshape(rows, width, size)
        slope[:, :, cut] = (sig * (1.0 + pre * (1.0 - sig)) * scale[:, cut]).reshape(rows, width, size)


def prepare(
    image, scale1, shift1, scale2, shift2, pairing, index, strip, near_send, far_send, vectors, pair, sems, *, table
):
    copies = [
        pltpu.make_async_copy(image, strip, sems.at[0]),
        pltpu.make_async_copy(pairing, pair, sems.at[1]),
    ]
    for i, source in enumerate((scale1, shift1, scale2, shift2)):
        copies.append(pltpu.make_async_copy(source, vectors.at[pl.ds(8 * i, 1)], sems.at[2 + i]))
    for copy in copies:
        copy.start()
    copies[1].wait()
    rank = jnp.int32(0)
    if table:
        groups = pair.shape[0]
        for i in range(groups):
            smaller = jnp.int32(0)
            for j in range(i + 1, groups):
                smaller = smaller + (pair[j] < pair[i]).astype(jnp.int32)
            rank = rank + smaller * math.factorial(groups - 1 - i)
        rank = lookup(rank, table)
    index[0] = rank
    me = lax.axis_index("peer")
    paired = jnp.where(pair[me] == me, 0.0, 1.0)
    vectors[pl.ds(32, 1)] = jnp.full((1, vectors.shape[1]), paired, F32)
    odd = side()
    edge = near_send.shape[0]
    last = strip.shape[0] - edge
    copies[0].wait()
    near_send[...] = strip[pl.ds(pick(odd, last, 0), edge)]
    far_send[...] = strip[pl.ds(pick(odd, 0, last), edge)]
    for copy in copies[2:]:
        copy.wait()


def first(image, near, kernel1, vectors, hidden, slope, cat):
    odd = side()
    strip, edge = image.shape[0], near.shape[0]
    put(cat, pick(odd, 0, edge), strip, image[...], D1)
    put(cat, pick(odd, strip, 0), edge, near[...], D1)
    conv_act(cat, kernel1, vectors[0:1], vectors[8:9], D1, hidden, slope)


def second(
    image, far, hidden, slope, kernel1, kernel2, vectors, task,
    feat_far, base_far, rate_far, feat_near, base_near, rate_near, fold,
    cat1, cat2, rim, slope1, slope2, part, feat, sems
):
    odd = side()
    strip, edge, held = image.shape[0], far.shape[0], hidden.shape[0]
    most = held - D1
    copies = [
        pltpu.make_async_copy(task, part, sems.at[0]),
        pltpu.make_async_copy(
            slope.at[pl.ds(pick(odd, 0, D1), most)], fold.at[pl.ds(pick(odd, D2, 0), most)], sems.at[1]
        ),
        pltpu.make_async_copy(
            slope1.at[pl.ds(pick(odd, D1, 0), D2)], fold.at[pl.ds(pick(odd, 0, most), D2)], sems.at[2]
        ),
    ]
    copies[0].start()
    copies[1].start()
    own = 2 * D1
    put_far(cat1, pick(odd, 0, own), far, D1)
    put(cat1, pick(odd, edge, 0), own, image[pl.ds(pick(odd, 0, strip - own), own)], D1)
    conv_act(cat1, kernel1, vectors[0:1], vectors[8:9], D1, rim, slope1)
    copies[2].start()
    hide_beyond(rim, odd, D2)
    put(cat2, pick(odd, edge, 0), held, hidden[...], D2)
    put(cat2, pick(odd, 0, held), edge, rim[...], D2)
    conv_act(cat2, kernel2, vectors[16:17], vectors[24:25], D2, feat, slope2)
    for copy in copies:
        copy.wait()
    paired = vectors[32:33]
    far_at = pl.ds(pick(odd, 0, strip - edge), edge)
    near_at = pl.ds(pick(odd, edge, 0), strip - edge)
    for at, own, base, rate in ((far_at, feat_far, base_far, rate_far), (near_at, feat_near, base_near, rate_near)):
        own[...] = feat[at]
        rate[...] = slope2[at] * paired
        base[...] = (part[at].astype(F32) + feat[at].astype(F32) * paired) * slope2[at]


def gradient(base, rate, partner, grad):
    def step(row, carry):
        grad[row] = (base[row] - partner[row].astype(F32) * rate[row]).astype(BF16)
        return carry

    lax.fori_loop(0, grad.shape[0], step, 0, unroll=2)


def grad_rest(base, rate, partner, grad_far, far, grads, near_send):
    odd = side()
    rows, edge = partner.shape[0], grad_far.shape[0]
    gradient(base, rate, partner, grads.at[pl.ds(pick(odd, 2 * edge, 0), rows)])
    grads[pl.ds(pick(odd, edge, rows), edge)] = grad_far[...]
    beyond = pl.ds(pick(odd, 0, edge + rows), edge)
    grads[beyond] = far[...]

    @pl.when(at_end())
    def _():
        grads[beyond] = jnp.zeros(far.shape, far.dtype)

    near_send[...] = grads[pl.ds(pick(odd, edge + rows, 0), edge)]


def bring(kernel2, kernel1, fold, kept2, kept1, slope, sems):
    pairs = ((kernel2, kept2), (kernel1, kept1), (fold, slope))
    copies = [pltpu.make_async_copy(source, target, sems.at[i]) for i, (source, target) in enumerate(pairs)]
    for copy in copies:
        copy.start()
    for copy in copies:
        copy.wait()


def backward(near, grads, fold, kernel2, kernel1, out, cat2, cat1, grad1):
    odd = side()
    edge, held, width, rows = near.shape[0], grads.shape[0], near.shape[1], grad1.shape[0]
    put(cat2, pick(odd, held, 0), edge, near[...], D2)
    put(cat2, pick(odd, 0, edge), held, grads[...], D2)
    for lo, size in halves(grad1.shape[2]):
        cut = slice(lo, lo + size)
        back = conv_t(cat2, kernel2, D2, rows, lo, size).reshape(rows, width, size)
        grad1[:, :, cut] = (back * fold[:, :, cut]).astype(BF16)
    hide_beyond(grad1, odd, D1)
    put(cat1, 0, rows, grad1[...], D1)
    rows = out.shape[0]
    for lo, size in halves(out.shape[2]):
        back = conv_t(cat1, kernel1, D1, rows, lo, size)
        out[:, :, lo : lo + size] = back.astype(BF16).reshape(rows, width, size)


def call(body, name, args, outs, scratch=(), flops=0, remote=(), stored=(), result=None):
    kinds = [pltpu.HBM if i in remote else pltpu.VMEM for i in range(len(args))]
    out_kinds = [
        pltpu.HBM if i in stored else pltpu.SMEM if o.dtype == jnp.int32 else pltpu.VMEM for i, o in enumerate(outs)
    ]
    return pl.pallas_call(
        body,
        out_shape=[o if i == result else k(o.shape, o.dtype) for i, (o, k) in enumerate(zip(outs, out_kinds))],
        in_specs=[pl.BlockSpec(memory_space=k) for k in kinds],
        out_specs=[pl.BlockSpec(memory_space=k) for k in out_kinds],
        scratch_shapes=[pltpu.VMEM(s.shape, s.dtype) if isinstance(s, jax.ShapeDtypeStruct) else s for s in scratch],
        compiler_params=pltpu.CompilerParams(vmem_limit_bytes=VMEM_LIMIT),
        cost_estimate=pl.CostEstimate(flops=flops, bytes_accessed=0, transcendentals=0),
        name=name,
    )(*[pltpu.with_memory_space_constraint(a, k) for a, k in zip(args, kinds)])


def routes_of(groups):
    pairings = list(itertools.permutations(range(groups)))
    moves = [frozenset((p, n) for n, p in enumerate(pair) if p != n) for pair in pairings]
    routes = []
    for move in sorted(set(moves), key=lambda m: (-len(m), sorted(m))):
        if not any(move <= route for route in routes):
            routes.append(move)
    chosen = [next(i for i, route in enumerate(routes) if move <= route) for move in moves]
    return [sorted(route) for route in routes], chosen


def spread(route, groups, space):
    moved = {source: target for source, target in route}
    return [
        (p * space + i, moved[p] * space + i if p in moved else p * space + (i ^ 1))
        for p in range(groups)
        for i in range(space)
    ]


def lookup(index, table):
    value = jnp.int32(table[0])
    for i in range(1, len(table)):
        if table[i] != table[i - 1]:
            value = jnp.where(index >= i, jnp.int32(table[i]), value)
    return value


def far_side(group, place, groups, space):
    other = place + 1 if place % 2 else place - 1
    if 0 <= other < space:
        return group * space + other
    return (group ^ 1) * space + place if groups % 2 == 0 else group * space + other % space


def swap_blocks(feat, pairing):
    groups = lax.axis_size("peer")
    chans = feat.shape[-1]
    blocks = feat.reshape(groups, feat.size // chans // groups, chans)
    received = lax.all_to_all(blocks, "peer", split_axis=0, concat_axis=0, tiled=True)
    chosen = jnp.take(received, pairing, axis=0)
    returned = lax.all_to_all(chosen, "peer", split_axis=0, concat_axis=0, tiled=True)
    return returned.reshape(feat.shape)


def per_device(images, task_grad, pairing, first_kernel, scale1, shift1, second_kernel, scale2, shift2):
    image, task = images[0], task_grad[0]
    strip, width, chans = image.shape
    kernel1 = first_kernel[0].reshape(3, 3 * chans, chans)
    kernel2 = second_kernel[0].reshape(3, 3 * chans, chans)
    space, groups = lax.axis_size("space"), lax.axis_size("peer")
    pairs = [(i, i ^ 1) for i in range(space)]
    across = [(p * space + i, far_side(p, i, groups, space)) for p in range(groups) for i in range(space)]
    per_row = 2 * 9 * width * chans * chans
    deep = strip + EDGE - 2 * D1

    def rows_of(count, kind=BF16):
        return jax.ShapeDtypeStruct((count, width, chans), kind)

    def cat_of(count):
        return jax.ShapeDtypeStruct((count, width, 3 * chans), BF16)

    def near(rows):
        return lax.ppermute(rows, "space", pairs)

    def far(rows):
        return lax.ppermute(rows, ("peer", "space"), across)

    routed = math.factorial(groups) <= MAX_ROUTES
    routes, chosen = routes_of(groups) if routed else ((), ())
    dma = pltpu.SemaphoreType.DMA
    index, image, near_send, far_send, vectors = call(
        functools.partial(prepare, table=tuple(chosen)),
        "prepare",
        (image, scale1, shift1, scale2, shift2, pairing),
        (
            jax.ShapeDtypeStruct((1,), jnp.int32),
            rows_of(strip),
            rows_of(EDGE),
            rows_of(EDGE),
            jax.ShapeDtypeStruct((40, chans), F32),
        ),
        (pltpu.SMEM((groups,), jnp.int32), dma((6,))),
        flops=LULL * per_row * strip,
        remote=range(6),
    )
    near_halo = near(near_send)
    far_halo = far(far_send)
    hidden, slope1 = call(
        first,
        "first",
        (image, near_halo, kernel1, vectors),
        (rows_of(deep), rows_of(deep, F32)),
        (cat_of(strip + EDGE),),
        flops=per_row * deep,
    )
    inner = strip - EDGE
    *given, fold = call(
        second,
        "second",
        (image, far_halo, hidden, slope1, kernel1, kernel2, vectors, task),
        (
            rows_of(EDGE),
            rows_of(EDGE, F32),
            rows_of(EDGE, F32),
            rows_of(inner),
            rows_of(inner, F32),
            rows_of(inner, F32),
            rows_of(strip + 2 * D1, F32),
        ),
        (
            cat_of(EDGE + 2 * D1),
            cat_of(strip + 2 * D2),
            rows_of(EDGE),
            rows_of(EDGE, F32),
            rows_of(strip, F32),
            rows_of(strip),
            rows_of(strip),
            dma((3,)),
        ),
        flops=per_row * (EDGE + strip),
        remote=(7,),
        stored=(6,),
    )

    whole = jax.ShapeDtypeStruct(kernel1.shape, BF16)

    def exchange(swap, feat_far, base_far, rate_far, feat_near, base_near, rate_near, *stored):
        partner_far = swap(feat_far)
        partner_near = swap(feat_near)
        (grad_far,) = call(gradient, "grad_far", (base_far, rate_far, partner_far), (rows_of(EDGE),))
        far_grad = far(grad_far)
        grads, near_send = call(
            grad_rest,
            "grad_rest",
            (base_near, rate_near, partner_near, grad_far, far_grad),
            (rows_of(strip + EDGE), rows_of(EDGE)),
        )
        brought = call(
            bring, "bring", stored, (whole, whole, rows_of(strip + 2 * D1, F32)), (dma((3,)),), remote=range(3)
        )
        return grads, near_send, *brought

    if routed:
        moves = [
            functools.partial(lax.ppermute, axis_name=("peer", "space"), perm=spread(route, groups, space))
            for route in routes
        ]
        state = lax.switch(index[0], [functools.partial(exchange, move) for move in moves], *given, kernel2, kernel1, fold)
    else:
        state = exchange(functools.partial(swap_blocks, pairing=pairing), *given, kernel2, kernel1, fold)
    grads, near_send, kernel2, kernel1, fold = state
    near_grad = near(near_send)
    back = strip + 2 * D1
    (out,) = call(
        backward,
        "backward",
        (near_grad, grads, fold, kernel2, kernel1),
        (rows_of(strip),),
        (cat_of(strip + 2 * EDGE), cat_of(back), rows_of(back)),
        flops=per_row * (back + strip),
        result=0,
    )
    return out[None]


def solution(mesh):
    placed = (
        P("peer", "space", None, None),
        P("peer", "space", None, None),
        P(),
        P("peer", None, None, None, None),
        P("peer", None),
        P("peer", None),
        P("peer", None, None, None, None),
        P("peer", None),
        P("peer", None),
    )
    return jax.shard_map(
        per_device,
        mesh=mesh,
        in_specs=placed,
        out_specs=P("peer", "space", None, None),
        check_vma=False,
    )
```

```python
import functools
import itertools
import math

import jax
import jax.numpy as jnp
from jax import lax
from jax.experimental import pallas as pl
from jax.experimental.pallas import tpu as pltpu
from jax.sharding import PartitionSpec as P

BF16 = jnp.bfloat16
F32 = jnp.float32
VMEM_LIMIT = 40 * 2**20
MAX_ROUTES = 24
LULL = 30
D1 = 2
D2 = 4
EDGE = D1 + D2


def side():
    return lax.rem(lax.axis_index("space"), 2)


def at_end():
    me = lax.axis_index("space")
    return jnp.logical_or(me == 0, me == lax.axis_size("space") - 1)


def pick(odd, if_even, if_odd):
    return if_even + odd * (if_odd - if_even)


def put(cat, start, rows, value, dilation):
    width, chans = value.shape[1], value.shape[2]
    none = jnp.zeros((rows, dilation, chans), value.dtype)
    at = pl.ds(start, rows)
    cat[at, :, 0:chans] = jnp.concatenate([none, value[:, : width - dilation]], axis=1)
    cat[at, :, chans : 2 * chans] = value
    cat[at, :, 2 * chans : 3 * chans] = jnp.concatenate([value[:, dilation:], none], axis=1)


def no_wait(*tap):
    pass


def conv(cat, kernel, dilation, rows, lo, size):
    width, depth = cat.shape[1], cat.shape[2]
    total = None
    for a in range(3):
        block = cat[a * dilation : a * dilation + rows].reshape(rows * width, depth)
        part = jnp.dot(block, kernel[a, :, lo : lo + size], preferred_element_type=F32)
        total = part if total is None else total + part
    return total


def conv_t(cat, kernel, dilation, rows, lo, size):
    width, chans = cat.shape[1], cat.shape[2] // 3
    total = None
    for a in range(3):
        for b in range(3):
            block = cat[(2 - a) * dilation : (2 - a) * dilation + rows, :, (2 - b) * chans : (3 - b) * chans]
            part = lax.dot_general(
                block.reshape(rows * width, chans),
                kernel[a, b * chans + lo : b * chans + lo + size],
                (((1,), (1,)), ((), ())),
                preferred_element_type=F32,
            )
            total = part if total is None else total + part
    return total


def hide_beyond(rim, odd, count):
    @pl.when(at_end())
    def _():
        none = jnp.zeros((count,) + rim.shape[1:], rim.dtype)
        rim[pl.ds(pick(odd, 0, rim.shape[0] - count), count)] = none


def put_far(cat, start, halo, dilation):
    rows = halo.shape[0]
    put(cat, start, rows, halo[...], dilation)

    @pl.when(at_end())
    def _():
        cat[pl.ds(start, rows)] = jnp.zeros((rows,) + cat.shape[1:], cat.dtype)


def halves(chans):
    step = chans // 2 if chans % 256 == 0 else chans
    return [(lo, step) for lo in range(0, chans, step)]


def conv_act(cat, kernel, scale, shift, dilation, act, slope):
    rows, width, chans = act.shape
    for lo, size in halves(chans):
        cut = slice(lo, lo + size)
        pre = conv(cat, kernel, dilation, rows, lo, size) * scale[:, cut] + shift[:, cut]
        sig = 1.0 / (1.0 + jnp.exp(-pre))
        act[:, :, cut] = (pre * sig).astype(BF16).reshape(rows, width, size)
        slope[:, :, cut] = (sig * (1.0 + pre * (1.0 - sig)) * scale[:, cut]).reshape(rows, width, size)


def prepare(
    image, scale1, shift1, scale2, shift2, pairing, index, strip, near_send, far_send, vectors, pair, sems, *, table
):
    copies = [
        pltpu.make_async_copy(image, strip, sems.at[0]),
        pltpu.make_async_copy(pairing, pair, sems.at[1]),
    ]
    for i, source in enumerate((scale1, shift1, scale2, shift2)):
        copies.append(pltpu.make_async_copy(source, vectors.at[pl.ds(8 * i, 1)], sems.at[2 + i]))
    for copy in copies:
        copy.start()
    copies[1].wait()
    rank = jnp.int32(0)
    if table:
        groups = pair.shape[0]
        for i in range(groups):
            smaller = jnp.int32(0)
            for j in range(i + 1, groups):
                smaller = smaller + (pair[j] < pair[i]).astype(jnp.int32)
            rank = rank + smaller * math.factorial(groups - 1 - i)
        rank = lookup(rank, table)
    index[0] = rank
    me = lax.axis_index("peer")
    paired = jnp.where(pair[me] == me, 0.0, 1.0)
    vectors[pl.ds(32, 1)] = jnp.full((1, vectors.shape[1]), paired, F32)
    odd = side()
    edge = near_send.shape[0]
    last = strip.shape[0] - edge
    copies[0].wait()
    near_send[...] = strip[pl.ds(pick(odd, last, 0), edge)]
    far_send[...] = strip[pl.ds(pick(odd, 0, last), edge)]
    for copy in copies[2:]:
        copy.wait()


def first(image, near, kernel1, vectors, hidden, slope, cat):
    odd = side()
    strip, edge = image.shape[0], near.shape[0]
    put(cat, pick(odd, 0, edge), strip, image[...], D1)
    put(cat, pick(odd, strip, 0), edge, near[...], D1)
    conv_act(cat, kernel1, vectors[0:1], vectors[8:9], D1, hidden, slope)


def second(
    image, far, hidden, slope, kernel1, kernel2, vectors, task,
    task_far, feat_far, slope_far, task_near, feat_near, slope_near, fold,
    cat1, cat2, rim, slope1, slope2, feat, sems
):
    odd = side()
    strip, edge, held = image.shape[0], far.shape[0], hidden.shape[0]
    most = held - D1
    far_at = pl.ds(pick(odd, 0, strip - edge), edge)
    near_at = pl.ds(pick(odd, edge, 0), strip - edge)
    copies = [
        pltpu.make_async_copy(task.at[far_at], task_far, sems.at[0]),
        pltpu.make_async_copy(
            slope.at[pl.ds(pick(odd, 0, D1), most)], fold.at[pl.ds(pick(odd, D2, 0), most)], sems.at[1]
        ),
        pltpu.make_async_copy(
            slope1.at[pl.ds(pick(odd, D1, 0), D2)], fold.at[pl.ds(pick(odd, 0, most), D2)], sems.at[2]
        ),
        pltpu.make_async_copy(task.at[near_at], task_near, sems.at[3]),
    ]
    copies[0].start()
    copies[1].start()
    copies[3].start()
    own = 2 * D1
    put_far(cat1, pick(odd, 0, own), far, D1)
    put(cat1, pick(odd, edge, 0), own, image[pl.ds(pick(odd, 0, strip - own), own)], D1)
    conv_act(cat1, kernel1, vectors[0:1], vectors[8:9], D1, rim, slope1)
    copies[2].start()
    hide_beyond(rim, odd, D2)
    put(cat2, pick(odd, edge, 0), held, hidden[...], D2)
    put(cat2, pick(odd, 0, held), edge, rim[...], D2)
    conv_act(cat2, kernel2, vectors[16:17], vectors[24:25], D2, feat, slope2)
    for copy in copies:
        copy.wait()
    for at, part, rate in ((far_at, feat_far, slope_far), (near_at, feat_near, slope_near)):
        part[...] = feat[at]
        rate[...] = slope2[at]


def gradient(task, feat, slope, partner, vectors, grad):
    paired = vectors[32:33]

    def step(row, carry):
        apart = (feat[row].astype(F32) - partner[row].astype(F32)) * paired
        grad[row] = ((task[row].astype(F32) + apart) * slope[row]).astype(BF16)
        return carry

    lax.fori_loop(0, grad.shape[0], step, 0, unroll=2)


def grad_first(task, feat, slope, partner, vectors, mark, grad):
    gradient(task, feat, slope, partner, vectors, grad)


def grad_rest(task, feat, slope, partner, vectors, grad_far, far, grads, near_send):
    odd = side()
    rows, edge = partner.shape[0], grad_far.shape[0]
    gradient(task, feat, slope, partner, vectors, grads.at[pl.ds(pick(odd, 2 * edge, 0), rows)])
    grads[pl.ds(pick(odd, edge, rows), edge)] = grad_far[...]
    beyond = pl.ds(pick(odd, 0, edge + rows), edge)
    grads[beyond] = far[...]

    @pl.when(at_end())
    def _():
        grads[beyond] = jnp.zeros(far.shape, far.dtype)

    near_send[...] = grads[pl.ds(pick(odd, edge + rows, 0), edge)]


def bring(kernel2, kernel1, fold, kept2, kept1, slope, mark, sems):
    pairs = ((kernel2, kept2), (kernel1, kept1), (fold, slope))
    copies = [pltpu.make_async_copy(source, target, sems.at[i]) for i, (source, target) in enumerate(pairs)]
    for copy in copies:
        copy.start()
    mark[...] = jnp.zeros_like(mark)
    for copy in copies:
        copy.wait()


def backward(near, grads, fold, kernel2, kernel1, out, cat2, cat1, grad1):
    odd = side()
    edge, held, width, rows = near.shape[0], grads.shape[0], near.shape[1], grad1.shape[0]
    put(cat2, pick(odd, held, 0), edge, near[...], D2)
    put(cat2, pick(odd, 0, edge), held, grads[...], D2)
    for lo, size in halves(grad1.shape[2]):
        cut = slice(lo, lo + size)
        back = conv_t(cat2, kernel2, D2, rows, lo, size).reshape(rows, width, size)
        grad1[:, :, cut] = (back * fold[:, :, cut]).astype(BF16)
    hide_beyond(grad1, odd, D1)
    put(cat1, 0, rows, grad1[...], D1)
    rows = out.shape[0]
    for lo, size in halves(out.shape[2]):
        back = conv_t(cat1, kernel1, D1, rows, lo, size)
        out[:, :, lo : lo + size] = back.astype(BF16).reshape(rows, width, size)


def call(body, name, args, outs, scratch=(), flops=0, remote=(), stored=(), result=None):
    kinds = [pltpu.HBM if i in remote else pltpu.VMEM for i in range(len(args))]
    out_kinds = [
        pltpu.HBM if i in stored else pltpu.SMEM if o.dtype == jnp.int32 else pltpu.VMEM for i, o in enumerate(outs)
    ]
    return pl.pallas_call(
        body,
        out_shape=[o if i == result else k(o.shape, o.dtype) for i, (o, k) in enumerate(zip(outs, out_kinds))],
        in_specs=[pl.BlockSpec(memory_space=k) for k in kinds],
        out_specs=[pl.BlockSpec(memory_space=k) for k in out_kinds],
        scratch_shapes=[pltpu.VMEM(s.shape, s.dtype) if isinstance(s, jax.ShapeDtypeStruct) else s for s in scratch],
        compiler_params=pltpu.CompilerParams(vmem_limit_bytes=VMEM_LIMIT),
        cost_estimate=pl.CostEstimate(flops=flops, bytes_accessed=0, transcendentals=0),
        name=name,
    )(*[pltpu.with_memory_space_constraint(a, k) for a, k in zip(args, kinds)])


def routes_of(groups):
    pairings = list(itertools.permutations(range(groups)))
    moves = [frozenset((p, n) for n, p in enumerate(pair) if p != n) for pair in pairings]
    routes = []
    for move in sorted(set(moves), key=lambda m: (-len(m), sorted(m))):
        if not any(move <= route for route in routes):
            routes.append(move)
    chosen = [next(i for i, route in enumerate(routes) if move <= route) for move in moves]
    return [sorted(route) for route in routes], chosen


def spread(route, groups, space):
    moved = {source: target for source, target in route}
    return [
        (p * space + i, moved[p] * space + i if p in moved else p * space + (i ^ 1))
        for p in range(groups)
        for i in range(space)
    ]


def lookup(index, table):
    value = jnp.int32(table[0])
    for i in range(1, len(table)):
        if table[i] != table[i - 1]:
            value = jnp.where(index >= i, jnp.int32(table[i]), value)
    return value


def far_side(group, place, groups, space):
    other = place + 1 if place % 2 else place - 1
    if 0 <= other < space:
        return group * space + other
    return (group ^ 1) * space + place if groups % 2 == 0 else group * space + other % space


def swap_blocks(feat, pairing):
    groups = lax.axis_size("peer")
    chans = feat.shape[-1]
    blocks = feat.reshape(groups, feat.size // chans // groups, chans)
    received = lax.all_to_all(blocks, "peer", split_axis=0, concat_axis=0, tiled=True)
    chosen = jnp.take(received, pairing, axis=0)
    returned = lax.all_to_all(chosen, "peer", split_axis=0, concat_axis=0, tiled=True)
    return returned.reshape(feat.shape)


def per_device(images, task_grad, pairing, first_kernel, scale1, shift1, second_kernel, scale2, shift2):
    image, task = images[0], task_grad[0]
    strip, width, chans = image.shape
    kernel1 = first_kernel[0].reshape(3, 3 * chans, chans)
    kernel2 = second_kernel[0].reshape(3, 3 * chans, chans)
    space, groups = lax.axis_size("space"), lax.axis_size("peer")
    pairs = [(i, i ^ 1) for i in range(space)]
    across = [(p * space + i, far_side(p, i, groups, space)) for p in range(groups) for i in range(space)]
    inside = [(p * space + i, p * space + (i + 1 if i % 2 else i - 1)) for p in range(groups) for i in range(1, space - 1)]
    per_row = 2 * 9 * width * chans * chans
    deep = strip + EDGE - 2 * D1

    def rows_of(count, kind=BF16):
        return jax.ShapeDtypeStruct((count, width, chans), kind)

    def cat_of(count):
        return jax.ShapeDtypeStruct((count, width, 3 * chans), BF16)

    def near(rows):
        return lax.ppermute(rows, "space", pairs)

    def far(rows, pairs):
        return lax.ppermute(rows, ("peer", "space"), pairs)

    routed = math.factorial(groups) <= MAX_ROUTES
    routes, chosen = routes_of(groups) if routed else ((), ())
    dma = pltpu.SemaphoreType.DMA
    index, image, near_send, far_send, vectors = call(
        functools.partial(prepare, table=tuple(chosen)),
        "prepare",
        (image, scale1, shift1, scale2, shift2, pairing),
        (
            jax.ShapeDtypeStruct((1,), jnp.int32),
            rows_of(strip),
            rows_of(EDGE),
            rows_of(EDGE),
            jax.ShapeDtypeStruct((40, chans), F32),
        ),
        (pltpu.SMEM((groups,), jnp.int32), dma((6,))),
        flops=LULL * per_row * strip,
        remote=range(6),
    )
    near_halo = near(near_send)
    far_halo = far(far_send, across)
    hidden, slope1 = call(
        first,
        "first",
        (image, near_halo, kernel1, vectors),
        (rows_of(deep), rows_of(deep, F32)),
        (cat_of(strip + EDGE),),
        flops=per_row * deep,
    )
    inner = strip - EDGE
    *given, fold = call(
        second,
        "second",
        (image, far_halo, hidden, slope1, kernel1, kernel2, vectors, task),
        (
            rows_of(EDGE),
            rows_of(EDGE),
            rows_of(EDGE, F32),
            rows_of(inner),
            rows_of(inner),
            rows_of(inner, F32),
            rows_of(strip + 2 * D1, F32),
        ),
        (
            cat_of(EDGE + 2 * D1),
            cat_of(strip + 2 * D2),
            rows_of(EDGE),
            rows_of(EDGE, F32),
            rows_of(strip, F32),
            rows_of(strip),
            dma((4,)),
        ),
        flops=per_row * (EDGE + strip),
        remote=(7,),
        stored=(6,),
    )

    whole = jax.ShapeDtypeStruct(kernel1.shape, BF16)

    def exchange(swap, task_far, feat_far, slope_far, task_near, feat_near, slope_near, vectors, *stored):
        partner_far = swap(feat_far)
        partner_near = swap(feat_near)
        *brought, mark = call(
            bring,
            "bring",
            stored,
            (whole, whole, rows_of(strip + 2 * D1, F32), jax.ShapeDtypeStruct((8, 128), F32)),
            (dma((3,)),),
            remote=range(3),
        )
        (grad_far,) = call(
            grad_first,
            "grad_first",
            (task_far, feat_far, slope_far, partner_far, vectors, mark),
            (rows_of(EDGE),),
        )
        far_grad = far(grad_far, inside)
        grads, near_send = call(
            grad_rest,
            "grad_rest",
            (task_near, feat_near, slope_near, partner_near, vectors, grad_far, far_grad),
            (rows_of(strip + EDGE), rows_of(EDGE)),
        )
        return grads, near_send, *brought

    if routed:
        moves = [
            functools.partial(lax.ppermute, axis_name=("peer", "space"), perm=spread(route, groups, space))
            for route in routes
        ]
        state = lax.switch(index[0], [functools.partial(exchange, move) for move in moves], *given, vectors, kernel2, kernel1, fold)
    else:
        state = exchange(functools.partial(swap_blocks, pairing=pairing), *given, vectors, kernel2, kernel1, fold)
    grads, near_send, kernel2, kernel1, fold = state
    near_grad = near(near_send)
    back = strip + 2 * D1
    (out,) = call(
        backward,
        "backward",
        (near_grad, grads, fold, kernel2, kernel1),
        (rows_of(strip),),
        (cat_of(strip + 2 * EDGE), cat_of(back), rows_of(back)),
        flops=per_row * (back + strip),
        result=0,
    )
    return out[None]


def solution(mesh):
    placed = (
        P("peer", "space", None, None),
        P("peer", "space", None, None),
        P(),
        P("peer", None, None, None, None),
        P("peer", None),
        P("peer", None),
        P("peer", None, None, None, None),
        P("peer", None),
        P("peer", None),
    )
    return jax.shard_map(
        per_device,
        mesh=mesh,
        in_specs=placed,
        out_specs=P("peer", "space", None, None),
        check_vma=False,
    )
```

```python
import functools
import itertools
import math

import jax
import jax.numpy as jnp
from jax import lax
from jax.experimental import pallas as pl
from jax.experimental.pallas import tpu as pltpu
from jax.sharding import PartitionSpec as P

BF16 = jnp.bfloat16
F32 = jnp.float32
VMEM_LIMIT = 40 * 2**20
MAX_ROUTES = 24
LULL = 30
D1 = 2
D2 = 4
EDGE = D1 + D2


def side():
    return lax.rem(lax.axis_index("space"), 2)


def at_end():
    me = lax.axis_index("space")
    return jnp.logical_or(me == 0, me == lax.axis_size("space") - 1)


def pick(odd, if_even, if_odd):
    return if_even + odd * (if_odd - if_even)


def put(cat, start, rows, value, dilation):
    width, chans = value.shape[1], value.shape[2]
    none = jnp.zeros((rows, dilation, chans), value.dtype)
    at = pl.ds(start, rows)
    cat[at, :, 0:chans] = jnp.concatenate([none, value[:, : width - dilation]], axis=1)
    cat[at, :, chans : 2 * chans] = value
    cat[at, :, 2 * chans : 3 * chans] = jnp.concatenate([value[:, dilation:], none], axis=1)


def no_wait(*tap):
    pass


def conv(cat, kernel, dilation, rows, lo, size):
    width, depth = cat.shape[1], cat.shape[2]
    total = None
    for a in range(3):
        block = cat[a * dilation : a * dilation + rows].reshape(rows * width, depth)
        part = jnp.dot(block, kernel[a, :, lo : lo + size], preferred_element_type=F32)
        total = part if total is None else total + part
    return total


def conv_t(cat, kernel, dilation, rows, lo, size):
    width, chans = cat.shape[1], cat.shape[2] // 3
    total = None
    for a in range(3):
        for b in range(3):
            block = cat[(2 - a) * dilation : (2 - a) * dilation + rows, :, (2 - b) * chans : (3 - b) * chans]
            part = lax.dot_general(
                block.reshape(rows * width, chans),
                kernel[a, b * chans + lo : b * chans + lo + size],
                (((1,), (1,)), ((), ())),
                preferred_element_type=F32,
            )
            total = part if total is None else total + part
    return total


def hide_beyond(rim, odd, count):
    @pl.when(at_end())
    def _():
        none = jnp.zeros((count,) + rim.shape[1:], rim.dtype)
        rim[pl.ds(pick(odd, 0, rim.shape[0] - count), count)] = none


def put_far(cat, start, halo, dilation):
    rows = halo.shape[0]
    put(cat, start, rows, halo[...], dilation)

    @pl.when(at_end())
    def _():
        cat[pl.ds(start, rows)] = jnp.zeros((rows,) + cat.shape[1:], cat.dtype)


def halves(chans):
    step = chans // 2 if chans % 256 == 0 else chans
    return [(lo, step) for lo in range(0, chans, step)]


def conv_act(cat, kernel, scale, shift, dilation, act, slope):
    rows, width, chans = act.shape
    for lo, size in halves(chans):
        cut = slice(lo, lo + size)
        pre = conv(cat, kernel, dilation, rows, lo, size) * scale[:, cut] + shift[:, cut]
        sig = 1.0 / (1.0 + jnp.exp(-pre))
        act[:, :, cut] = (pre * sig).astype(BF16).reshape(rows, width, size)
        slope[:, :, cut] = (sig * (1.0 + pre * (1.0 - sig)) * scale[:, cut]).reshape(rows, width, size)


def prepare(
    image, scale1, shift1, scale2, shift2, pairing, index, strip, near_send, far_send, vectors, pair, sems, *, table
):
    copies = [
        pltpu.make_async_copy(image, strip, sems.at[0]),
        pltpu.make_async_copy(pairing, pair, sems.at[1]),
    ]
    for i, source in enumerate((scale1, shift1, scale2, shift2)):
        copies.append(pltpu.make_async_copy(source, vectors.at[pl.ds(8 * i, 1)], sems.at[2 + i]))
    for copy in copies:
        copy.start()
    copies[1].wait()
    rank = jnp.int32(0)
    if table:
        groups = pair.shape[0]
        for i in range(groups):
            smaller = jnp.int32(0)
            for j in range(i + 1, groups):
                smaller = smaller + (pair[j] < pair[i]).astype(jnp.int32)
            rank = rank + smaller * math.factorial(groups - 1 - i)
        rank = lookup(rank, table)
    index[0] = rank
    me = lax.axis_index("peer")
    paired = jnp.where(pair[me] == me, 0.0, 1.0)
    vectors[pl.ds(32, 1)] = jnp.full((1, vectors.shape[1]), paired, F32)
    odd = side()
    edge = near_send.shape[0]
    last = strip.shape[0] - edge
    copies[0].wait()
    near_send[...] = strip[pl.ds(pick(odd, last, 0), edge)]
    far_send[...] = strip[pl.ds(pick(odd, 0, last), edge)]
    for copy in copies[2:]:
        copy.wait()


def first(image, near, kernel1, vectors, hidden, slope, cat):
    odd = side()
    strip, edge = image.shape[0], near.shape[0]
    put(cat, pick(odd, 0, edge), strip, image[...], D1)
    put(cat, pick(odd, strip, 0), edge, near[...], D1)
    conv_act(cat, kernel1, vectors[0:1], vectors[8:9], D1, hidden, slope)


def second(
    image, far, hidden, slope, kernel1, kernel2, vectors, task,
    task_far, feat_far, slope_far, task_near, feat_near, slope_near, task_mid, feat_mid, slope_mid, fold,
    cat1, cat2, rim, slope1, slope2, feat, sems
):
    odd = side()
    strip, edge, held = image.shape[0], far.shape[0], hidden.shape[0]
    most = held - D1
    far_at = pl.ds(pick(odd, 0, strip - edge), edge)
    near_at = pl.ds(pick(odd, strip - edge, 0), edge)
    mid_at = pl.ds(edge, strip - 2 * edge)
    copies = [
        pltpu.make_async_copy(task.at[far_at], task_far, sems.at[0]),
        pltpu.make_async_copy(
            slope.at[pl.ds(pick(odd, 0, D1), most)], fold.at[pl.ds(pick(odd, D2, 0), most)], sems.at[1]
        ),
        pltpu.make_async_copy(
            slope1.at[pl.ds(pick(odd, D1, 0), D2)], fold.at[pl.ds(pick(odd, 0, most), D2)], sems.at[2]
        ),
        pltpu.make_async_copy(task.at[near_at], task_near, sems.at[3]),
        pltpu.make_async_copy(task.at[mid_at], task_mid, sems.at[4]),
    ]
    for i in (0, 1, 3, 4):
        copies[i].start()
    own = 2 * D1
    put_far(cat1, pick(odd, 0, own), far, D1)
    put(cat1, pick(odd, edge, 0), own, image[pl.ds(pick(odd, 0, strip - own), own)], D1)
    conv_act(cat1, kernel1, vectors[0:1], vectors[8:9], D1, rim, slope1)
    copies[2].start()
    hide_beyond(rim, odd, D2)
    put(cat2, pick(odd, edge, 0), held, hidden[...], D2)
    put(cat2, pick(odd, 0, held), edge, rim[...], D2)
    conv_act(cat2, kernel2, vectors[16:17], vectors[24:25], D2, feat, slope2)
    for copy in copies:
        copy.wait()
    parts = ((far_at, feat_far, slope_far), (near_at, feat_near, slope_near), (mid_at, feat_mid, slope_mid))
    for at, part, rate in parts:
        part[...] = feat[at]
        rate[...] = slope2[at]


def gradient(task, feat, slope, partner, vectors, grad):
    paired = vectors[32:33]

    def step(row, carry):
        apart = (feat[row].astype(F32) - partner[row].astype(F32)) * paired
        grad[row] = ((task[row].astype(F32) + apart) * slope[row]).astype(BF16)
        return carry

    lax.fori_loop(0, grad.shape[0], step, 0, unroll=2)


def grad_first(task, feat, slope, partner, vectors, mark, grad):
    gradient(task, feat, slope, partner, vectors, grad)


def gather(far, grad_far, grad_mid, grad_near, near, grads):
    odd = side()
    edge, mid = far.shape[0], grad_mid.shape[0]
    beyond = pl.ds(pick(odd, 0, 3 * edge + mid), edge)
    grads[beyond] = far[...]

    @pl.when(at_end())
    def _():
        grads[beyond] = jnp.zeros(far.shape, far.dtype)

    grads[pl.ds(pick(odd, edge, 2 * edge + mid), edge)] = grad_far[...]
    grads[pl.ds(2 * edge, mid)] = grad_mid[...]
    grads[pl.ds(pick(odd, 2 * edge + mid, edge), edge)] = grad_near[...]
    grads[pl.ds(pick(odd, 3 * edge + mid, 0), edge)] = near[...]


def bring(kernel2, kernel1, fold, kept2, kept1, slope, mark, sems):
    pairs = ((kernel2, kept2), (kernel1, kept1), (fold, slope))
    copies = [pltpu.make_async_copy(source, target, sems.at[i]) for i, (source, target) in enumerate(pairs)]
    for copy in copies:
        copy.start()
    mark[...] = jnp.zeros_like(mark)
    for copy in copies:
        copy.wait()


def backward(grads, fold, kernel2, kernel1, out, cat2, cat1, grad1):
    width, rows = grads.shape[1], grad1.shape[0]
    put(cat2, 0, grads.shape[0], grads[...], D2)
    for lo, size in halves(grad1.shape[2]):
        cut = slice(lo, lo + size)
        back = conv_t(cat2, kernel2, D2, rows, lo, size).reshape(rows, width, size)
        grad1[:, :, cut] = (back * fold[:, :, cut]).astype(BF16)
    hide_beyond(grad1, side(), D1)
    put(cat1, 0, rows, grad1[...], D1)
    rows = out.shape[0]
    for lo, size in halves(out.shape[2]):
        back = conv_t(cat1, kernel1, D1, rows, lo, size)
        out[:, :, lo : lo + size] = back.astype(BF16).reshape(rows, width, size)


def call(body, name, args, outs, scratch=(), flops=0, remote=(), stored=(), result=None):
    kinds = [pltpu.HBM if i in remote else pltpu.VMEM for i in range(len(args))]
    out_kinds = [
        pltpu.HBM if i in stored else pltpu.SMEM if o.dtype == jnp.int32 else pltpu.VMEM for i, o in enumerate(outs)
    ]
    return pl.pallas_call(
        body,
        out_shape=[o if i == result else k(o.shape, o.dtype) for i, (o, k) in enumerate(zip(outs, out_kinds))],
        in_specs=[pl.BlockSpec(memory_space=k) for k in kinds],
        out_specs=[pl.BlockSpec(memory_space=k) for k in out_kinds],
        scratch_shapes=[pltpu.VMEM(s.shape, s.dtype) if isinstance(s, jax.ShapeDtypeStruct) else s for s in scratch],
        compiler_params=pltpu.CompilerParams(vmem_limit_bytes=VMEM_LIMIT),
        cost_estimate=pl.CostEstimate(flops=flops, bytes_accessed=0, transcendentals=0),
        name=name,
    )(*[pltpu.with_memory_space_constraint(a, k) for a, k in zip(args, kinds)])


def routes_of(groups):
    pairings = list(itertools.permutations(range(groups)))
    moves = [frozenset((p, n) for n, p in enumerate(pair) if p != n) for pair in pairings]
    routes = []
    for move in sorted(set(moves), key=lambda m: (-len(m), sorted(m))):
        if not any(move <= route for route in routes):
            routes.append(move)
    chosen = [next(i for i, route in enumerate(routes) if move <= route) for move in moves]
    return [sorted(route) for route in routes], chosen


def spread(route, groups, space):
    moved = {source: target for source, target in route}
    return [
        (p * space + i, moved[p] * space + i if p in moved else p * space + (i ^ 1))
        for p in range(groups)
        for i in range(space)
    ]


def lookup(index, table):
    value = jnp.int32(table[0])
    for i in range(1, len(table)):
        if table[i] != table[i - 1]:
            value = jnp.where(index >= i, jnp.int32(table[i]), value)
    return value


def far_side(group, place, groups, space):
    other = place + 1 if place % 2 else place - 1
    if 0 <= other < space:
        return group * space + other
    return (group ^ 1) * space + place if groups % 2 == 0 else group * space + other % space


def swap_blocks(feat, pairing):
    groups = lax.axis_size("peer")
    chans = feat.shape[-1]
    blocks = feat.reshape(groups, feat.size // chans // groups, chans)
    received = lax.all_to_all(blocks, "peer", split_axis=0, concat_axis=0, tiled=True)
    chosen = jnp.take(received, pairing, axis=0)
    returned = lax.all_to_all(chosen, "peer", split_axis=0, concat_axis=0, tiled=True)
    return returned.reshape(feat.shape)


def per_device(images, task_grad, pairing, first_kernel, scale1, shift1, second_kernel, scale2, shift2):
    image, task = images[0], task_grad[0]
    strip, width, chans = image.shape
    kernel1 = first_kernel[0].reshape(3, 3 * chans, chans)
    kernel2 = second_kernel[0].reshape(3, 3 * chans, chans)
    space, groups = lax.axis_size("space"), lax.axis_size("peer")
    pairs = [(i, i ^ 1) for i in range(space)]
    across = [(p * space + i, far_side(p, i, groups, space)) for p in range(groups) for i in range(space)]
    inside = [(p * space + i, p * space + (i + 1 if i % 2 else i - 1)) for p in range(groups) for i in range(1, space - 1)]
    per_row = 2 * 9 * width * chans * chans
    deep = strip + EDGE - 2 * D1

    def rows_of(count, kind=BF16):
        return jax.ShapeDtypeStruct((count, width, chans), kind)

    def cat_of(count):
        return jax.ShapeDtypeStruct((count, width, 3 * chans), BF16)

    def near(rows):
        return lax.ppermute(rows, "space", pairs)

    def far(rows, pairs):
        return lax.ppermute(rows, ("peer", "space"), pairs)

    routed = math.factorial(groups) <= MAX_ROUTES
    routes, chosen = routes_of(groups) if routed else ((), ())
    dma = pltpu.SemaphoreType.DMA
    index, image, near_send, far_send, vectors = call(
        functools.partial(prepare, table=tuple(chosen)),
        "prepare",
        (image, scale1, shift1, scale2, shift2, pairing),
        (
            jax.ShapeDtypeStruct((1,), jnp.int32),
            rows_of(strip),
            rows_of(EDGE),
            rows_of(EDGE),
            jax.ShapeDtypeStruct((40, chans), F32),
        ),
        (pltpu.SMEM((groups,), jnp.int32), dma((6,))),
        flops=LULL * per_row * strip,
        remote=range(6),
    )
    near_halo = near(near_send)
    far_halo = far(far_send, across)
    hidden, slope1 = call(
        first,
        "first",
        (image, near_halo, kernel1, vectors),
        (rows_of(deep), rows_of(deep, F32)),
        (cat_of(strip + EDGE),),
        flops=per_row * deep,
    )
    mid = strip - 2 * EDGE
    *given, fold = call(
        second,
        "second",
        (image, far_halo, hidden, slope1, kernel1, kernel2, vectors, task),
        (
            *[rows_of(count, kind) for count in (EDGE, EDGE, mid) for kind in (BF16, BF16, F32)],
            rows_of(strip + 2 * D1, F32),
        ),
        (
            cat_of(EDGE + 2 * D1),
            cat_of(strip + 2 * D2),
            rows_of(EDGE),
            rows_of(EDGE, F32),
            rows_of(strip, F32),
            rows_of(strip),
            dma((5,)),
        ),
        flops=per_row * (EDGE + strip),
        remote=(7,),
        stored=(9,),
    )

    whole = jax.ShapeDtypeStruct(kernel1.shape, BF16)

    def exchange(swap, *given):
        far_given, near_given, mid_given, (vectors, *stored) = given[:3], given[3:6], given[6:9], given[9:]
        partner_far, partner_near, partner_mid = swap(far_given[1]), swap(near_given[1]), swap(mid_given[1])
        *brought, mark = call(
            bring,
            "bring",
            stored,
            (whole, whole, rows_of(strip + 2 * D1, F32), jax.ShapeDtypeStruct((8, 128), F32)),
            (dma((3,)),),
            remote=range(3),
        )
        (grad_far,) = call(
            grad_first,
            "grad_first",
            (*far_given, partner_far, vectors, mark),
            (rows_of(EDGE),),
            flops=0 * per_row,
        )
        far_grad = far(grad_far, inside)
        (grad_near,) = call(
            grad_first,
            "grad_near",
            (*near_given, partner_near, vectors, grad_far),
            (rows_of(EDGE),),
            flops=0 * per_row,
        )
        (grad_mid,) = call(
            gradient, "grad_mid", (*mid_given, partner_mid, vectors), (rows_of(mid),), flops=18 * per_row
        )
        (grads,) = call(
            gather, "gather", (far_grad, grad_far, grad_mid, grad_near, near(grad_near)), (rows_of(strip + 2 * EDGE),)
        )
        return grads, *brought

    if routed:
        moves = [
            functools.partial(lax.ppermute, axis_name=("peer", "space"), perm=spread(route, groups, space))
            for route in routes
        ]
        state = lax.switch(index[0], [functools.partial(exchange, move) for move in moves], *given, vectors, kernel2, kernel1, fold)
    else:
        state = exchange(functools.partial(swap_blocks, pairing=pairing), *given, vectors, kernel2, kernel1, fold)
    grads, kernel2, kernel1, fold = state
    back = strip + 2 * D1
    (out,) = call(
        backward,
        "backward",
        (grads, fold, kernel2, kernel1),
        (rows_of(strip),),
        (cat_of(strip + 2 * EDGE), cat_of(back), rows_of(back)),
        flops=per_row * (back + strip),
        result=0,
    )
    return out[None]


def solution(mesh):
    placed = (
        P("peer", "space", None, None),
        P("peer", "space", None, None),
        P(),
        P("peer", None, None, None, None),
        P("peer", None),
        P("peer", None),
        P("peer", None, None, None, None),
        P("peer", None),
        P("peer", None),
    )
    return jax.shard_map(
        per_device,
        mesh=mesh,
        in_specs=placed,
        out_specs=P("peer", "space", None, None),
        check_vma=False,
    )
```

```python
import functools
import itertools
import math

import jax
import jax.numpy as jnp
from jax import lax
from jax.experimental import pallas as pl
from jax.experimental.pallas import tpu as pltpu
from jax.sharding import PartitionSpec as P

BF16 = jnp.bfloat16
F32 = jnp.float32
VMEM_LIMIT = 40 * 2**20
MAX_ROUTES = 24
LULL = 30
D1 = 2
D2 = 4
EDGE = D1 + D2


def side():
    return lax.rem(lax.axis_index("space"), 2)


def at_end():
    me = lax.axis_index("space")
    return jnp.logical_or(me == 0, me == lax.axis_size("space") - 1)


def pick(odd, if_even, if_odd):
    return if_even + odd * (if_odd - if_even)


def put(cat, start, rows, value, dilation):
    width, chans = value.shape[1], value.shape[2]
    none = jnp.zeros((rows, dilation, chans), value.dtype)
    at = pl.ds(start, rows)
    cat[at, :, 0:chans] = jnp.concatenate([none, value[:, : width - dilation]], axis=1)
    cat[at, :, chans : 2 * chans] = value
    cat[at, :, 2 * chans : 3 * chans] = jnp.concatenate([value[:, dilation:], none], axis=1)


def no_wait(*tap):
    pass


def conv(cat, kernel, dilation, rows, lo, size):
    width, depth = cat.shape[1], cat.shape[2]
    total = None
    for a in range(3):
        block = cat[a * dilation : a * dilation + rows].reshape(rows * width, depth)
        part = jnp.dot(block, kernel[a, :, lo : lo + size], preferred_element_type=F32)
        total = part if total is None else total + part
    return total


def conv_t(cat, kernel, dilation, rows, lo, size):
    width, chans = cat.shape[1], cat.shape[2] // 3
    total = None
    for a in range(3):
        for b in range(3):
            block = cat[(2 - a) * dilation : (2 - a) * dilation + rows, :, (2 - b) * chans : (3 - b) * chans]
            part = lax.dot_general(
                block.reshape(rows * width, chans),
                kernel[a, b * chans + lo : b * chans + lo + size],
                (((1,), (1,)), ((), ())),
                preferred_element_type=F32,
            )
            total = part if total is None else total + part
    return total


def hide_beyond(rim, odd, count):
    @pl.when(at_end())
    def _():
        none = jnp.zeros((count,) + rim.shape[1:], rim.dtype)
        rim[pl.ds(pick(odd, 0, rim.shape[0] - count), count)] = none


def put_far(cat, start, halo, dilation):
    rows = halo.shape[0]
    put(cat, start, rows, halo[...], dilation)

    @pl.when(at_end())
    def _():
        cat[pl.ds(start, rows)] = jnp.zeros((rows,) + cat.shape[1:], cat.dtype)


def halves(chans):
    step = chans // 2 if chans % 256 == 0 else chans
    return [(lo, step) for lo in range(0, chans, step)]


def conv_act(cat, kernel, scale, shift, dilation, act, slope):
    rows, width, chans = act.shape
    for lo, size in halves(chans):
        cut = slice(lo, lo + size)
        pre = conv(cat, kernel, dilation, rows, lo, size) * scale[:, cut] + shift[:, cut]
        sig = 1.0 / (1.0 + jnp.exp(-pre))
        act[:, :, cut] = (pre * sig).astype(BF16).reshape(rows, width, size)
        slope[:, :, cut] = (sig * (1.0 + pre * (1.0 - sig)) * scale[:, cut]).reshape(rows, width, size)


def prepare(
    image, scale1, shift1, scale2, shift2, pairing, index, strip, near_send, far_send, vectors, pair, sems, *, table
):
    copies = [
        pltpu.make_async_copy(image, strip, sems.at[0]),
        pltpu.make_async_copy(pairing, pair, sems.at[1]),
    ]
    for i, source in enumerate((scale1, shift1, scale2, shift2)):
        copies.append(pltpu.make_async_copy(source, vectors.at[pl.ds(8 * i, 1)], sems.at[2 + i]))
    for copy in copies:
        copy.start()
    copies[1].wait()
    rank = jnp.int32(0)
    if table:
        groups = pair.shape[0]
        for i in range(groups):
            smaller = jnp.int32(0)
            for j in range(i + 1, groups):
                smaller = smaller + (pair[j] < pair[i]).astype(jnp.int32)
            rank = rank + smaller * math.factorial(groups - 1 - i)
        rank = lookup(rank, table)
    index[0] = rank
    me = lax.axis_index("peer")
    paired = jnp.where(pair[me] == me, 0.0, 1.0)
    vectors[pl.ds(32, 1)] = jnp.full((1, vectors.shape[1]), paired, F32)
    odd = side()
    edge = near_send.shape[0]
    last = strip.shape[0] - edge
    copies[0].wait()
    near_send[...] = strip[pl.ds(pick(odd, last, 0), edge)]
    far_send[...] = strip[pl.ds(pick(odd, 0, last), edge)]
    for copy in copies[2:]:
        copy.wait()


def first(image, near, kernel1, vectors, hidden, slope, cat):
    odd = side()
    strip, edge = image.shape[0], near.shape[0]
    put(cat, pick(odd, 0, edge), strip, image[...], D1)
    put(cat, pick(odd, strip, 0), edge, near[...], D1)
    conv_act(cat, kernel1, vectors[0:1], vectors[8:9], D1, hidden, slope)


def second(
    image, far, hidden, slope, kernel1, kernel2, vectors, task,
    task_far, feat_far, slope_far, task_near, feat_near, slope_near, task_mid, feat_mid, slope_mid, fold,
    cat1, cat2, rim, slope1, slope2, feat, sems
):
    odd = side()
    strip, edge, held = image.shape[0], far.shape[0], hidden.shape[0]
    most = held - D1
    far_at = pl.ds(pick(odd, 0, strip - edge), edge)
    near_at = pl.ds(pick(odd, strip - edge, 0), edge)
    mid_at = pl.ds(edge, strip - 2 * edge)
    copies = [
        pltpu.make_async_copy(task.at[far_at], task_far, sems.at[0]),
        pltpu.make_async_copy(
            slope.at[pl.ds(pick(odd, 0, D1), most)], fold.at[pl.ds(pick(odd, D2, 0), most)], sems.at[1]
        ),
        pltpu.make_async_copy(
            slope1.at[pl.ds(pick(odd, D1, 0), D2)], fold.at[pl.ds(pick(odd, 0, most), D2)], sems.at[2]
        ),
        pltpu.make_async_copy(task.at[near_at], task_near, sems.at[3]),
        pltpu.make_async_copy(task.at[mid_at], task_mid, sems.at[4]),
    ]
    for i in (0, 1, 3, 4):
        copies[i].start()
    own = 2 * D1
    put_far(cat1, pick(odd, 0, own), far, D1)
    put(cat1, pick(odd, edge, 0), own, image[pl.ds(pick(odd, 0, strip - own), own)], D1)
    conv_act(cat1, kernel1, vectors[0:1], vectors[8:9], D1, rim, slope1)
    copies[2].start()
    hide_beyond(rim, odd, D2)
    put(cat2, pick(odd, edge, 0), held, hidden[...], D2)
    put(cat2, pick(odd, 0, held), edge, rim[...], D2)
    conv_act(cat2, kernel2, vectors[16:17], vectors[24:25], D2, feat, slope2)
    for copy in copies:
        copy.wait()
    parts = ((far_at, feat_far, slope_far), (near_at, feat_near, slope_near), (mid_at, feat_mid, slope_mid))
    for at, part, rate in parts:
        part[...] = feat[at]
        rate[...] = slope2[at]


def gradient(task, feat, slope, partner, vectors, grad):
    paired = vectors[32:33]

    def step(row, carry):
        apart = (feat[row].astype(F32) - partner[row].astype(F32)) * paired
        grad[row] = ((task[row].astype(F32) + apart) * slope[row]).astype(BF16)
        return carry

    lax.fori_loop(0, grad.shape[0], step, 0, unroll=2)


def grad_first(task, feat, slope, partner, vectors, mark, grad):
    gradient(task, feat, slope, partner, vectors, grad)


def gather(far, grad_far, grad_mid, grad_near, near, grads):
    odd = side()
    edge, mid = far.shape[0], grad_mid.shape[0]
    beyond = pl.ds(pick(odd, 0, 3 * edge + mid), edge)
    grads[beyond] = far[...]

    @pl.when(at_end())
    def _():
        grads[beyond] = jnp.zeros(far.shape, far.dtype)

    grads[pl.ds(pick(odd, edge, 2 * edge + mid), edge)] = grad_far[...]
    grads[pl.ds(2 * edge, mid)] = grad_mid[...]
    grads[pl.ds(pick(odd, 2 * edge + mid, edge), edge)] = grad_near[...]
    grads[pl.ds(pick(odd, 3 * edge + mid, 0), edge)] = near[...]


def bring(kernel2, kernel1, fold, kept2, kept1, slope, mark, sems):
    pairs = ((kernel2, kept2), (kernel1, kept1), (fold, slope))
    copies = [pltpu.make_async_copy(source, target, sems.at[i]) for i, (source, target) in enumerate(pairs)]
    for copy in copies:
        copy.start()
    mark[...] = jnp.zeros_like(mark)
    for copy in copies:
        copy.wait()


def backward(grads, fold, kernel2, kernel1, out, cat2, cat1, grad1):
    width, rows = grads.shape[1], grad1.shape[0]
    put(cat2, 0, grads.shape[0], grads[...], D2)
    for lo, size in halves(grad1.shape[2]):
        cut = slice(lo, lo + size)
        back = conv_t(cat2, kernel2, D2, rows, lo, size).reshape(rows, width, size)
        grad1[:, :, cut] = (back * fold[:, :, cut]).astype(BF16)
    hide_beyond(grad1, side(), D1)
    put(cat1, 0, rows, grad1[...], D1)
    rows = out.shape[0]
    for lo, size in halves(out.shape[2]):
        back = conv_t(cat1, kernel1, D1, rows, lo, size)
        out[:, :, lo : lo + size] = back.astype(BF16).reshape(rows, width, size)


def call(body, name, args, outs, scratch=(), flops=0, remote=(), stored=(), result=None):
    kinds = [pltpu.HBM if i in remote else pltpu.VMEM for i in range(len(args))]
    out_kinds = [
        pltpu.HBM if i in stored else pltpu.SMEM if o.dtype == jnp.int32 else pltpu.VMEM for i, o in enumerate(outs)
    ]
    return pl.pallas_call(
        body,
        out_shape=[o if i == result else k(o.shape, o.dtype) for i, (o, k) in enumerate(zip(outs, out_kinds))],
        in_specs=[pl.BlockSpec(memory_space=k) for k in kinds],
        out_specs=[pl.BlockSpec(memory_space=k) for k in out_kinds],
        scratch_shapes=[pltpu.VMEM(s.shape, s.dtype) if isinstance(s, jax.ShapeDtypeStruct) else s for s in scratch],
        compiler_params=pltpu.CompilerParams(vmem_limit_bytes=VMEM_LIMIT),
        cost_estimate=pl.CostEstimate(flops=flops, bytes_accessed=0, transcendentals=0),
        name=name,
    )(*[pltpu.with_memory_space_constraint(a, k) for a, k in zip(args, kinds)])


def routes_of(groups):
    pairings = list(itertools.permutations(range(groups)))
    moves = [frozenset((p, n) for n, p in enumerate(pair) if p != n) for pair in pairings]
    routes = []
    for move in sorted(set(moves), key=lambda m: (-len(m), sorted(m))):
        if not any(move <= route for route in routes):
            routes.append(move)
    chosen = [next(i for i, route in enumerate(routes) if move <= route) for move in moves]
    return [sorted(route) for route in routes], chosen


def spread(route, groups, space):
    moved = {source: target for source, target in route}
    return [
        (p * space + i, moved[p] * space + i if p in moved else p * space + (i ^ 1))
        for p in range(groups)
        for i in range(space)
    ]


def lookup(index, table):
    value = jnp.int32(table[0])
    for i in range(1, len(table)):
        if table[i] != table[i - 1]:
            value = jnp.where(index >= i, jnp.int32(table[i]), value)
    return value


def far_side(group, place, groups, space):
    other = place + 1 if place % 2 else place - 1
    if 0 <= other < space:
        return group * space + other
    return (group ^ 1) * space + place if groups % 2 == 0 else group * space + other % space


def swap_blocks(feat, pairing):
    groups = lax.axis_size("peer")
    chans = feat.shape[-1]
    blocks = feat.reshape(groups, feat.size // chans // groups, chans)
    received = lax.all_to_all(blocks, "peer", split_axis=0, concat_axis=0, tiled=True)
    chosen = jnp.take(received, pairing, axis=0)
    returned = lax.all_to_all(chosen, "peer", split_axis=0, concat_axis=0, tiled=True)
    return returned.reshape(feat.shape)


def per_device(images, task_grad, pairing, first_kernel, scale1, shift1, second_kernel, scale2, shift2):
    image, task = images[0], task_grad[0]
    strip, width, chans = image.shape
    kernel1 = first_kernel[0].reshape(3, 3 * chans, chans)
    kernel2 = second_kernel[0].reshape(3, 3 * chans, chans)
    space, groups = lax.axis_size("space"), lax.axis_size("peer")
    pairs = [(i, i ^ 1) for i in range(space)]
    across = [(p * space + i, far_side(p, i, groups, space)) for p in range(groups) for i in range(space)]
    inside = [(p * space + i, p * space + (i + 1 if i % 2 else i - 1)) for p in range(groups) for i in range(1, space - 1)]
    per_row = 2 * 9 * width * chans * chans
    deep = strip + EDGE - 2 * D1

    def rows_of(count, kind=BF16):
        return jax.ShapeDtypeStruct((count, width, chans), kind)

    def cat_of(count):
        return jax.ShapeDtypeStruct((count, width, 3 * chans), BF16)

    def near(rows):
        return lax.ppermute(rows, "space", pairs)

    def far(rows, pairs):
        return lax.ppermute(rows, ("peer", "space"), pairs)

    routed = math.factorial(groups) <= MAX_ROUTES
    routes, chosen = routes_of(groups) if routed else ((), ())
    dma = pltpu.SemaphoreType.DMA
    index, image, near_send, far_send, vectors = call(
        functools.partial(prepare, table=tuple(chosen)),
        "prepare",
        (image, scale1, shift1, scale2, shift2, pairing),
        (
            jax.ShapeDtypeStruct((1,), jnp.int32),
            rows_of(strip),
            rows_of(EDGE),
            rows_of(EDGE),
            jax.ShapeDtypeStruct((40, chans), F32),
        ),
        (pltpu.SMEM((groups,), jnp.int32), dma((6,))),
        flops=LULL * per_row * strip,
        remote=range(6),
    )
    near_halo = near(near_send)
    far_halo = far(far_send, across)
    hidden, slope1 = call(
        first,
        "first",
        (image, near_halo, kernel1, vectors),
        (rows_of(deep), rows_of(deep, F32)),
        (cat_of(strip + EDGE),),
        flops=per_row * deep,
    )
    mid = strip - 2 * EDGE
    *given, fold = call(
        second,
        "second",
        (image, far_halo, hidden, slope1, kernel1, kernel2, vectors, task),
        (
            *[rows_of(count, kind) for count in (EDGE, EDGE, mid) for kind in (BF16, BF16, F32)],
            rows_of(strip + 2 * D1, F32),
        ),
        (
            cat_of(EDGE + 2 * D1),
            cat_of(strip + 2 * D2),
            rows_of(EDGE),
            rows_of(EDGE, F32),
            rows_of(strip, F32),
            rows_of(strip),
            dma((5,)),
        ),
        flops=per_row * (EDGE + strip),
        remote=(7,),
        stored=(9,),
    )

    whole = jax.ShapeDtypeStruct(kernel1.shape, BF16)

    def exchange(swap, *given):
        far_given, near_given, mid_given, (vectors, *stored) = given[:3], given[3:6], given[6:9], given[9:]
        partner_far, partner_near = swap(far_given[1]), swap(near_given[1])
        *brought, mark = call(
            bring,
            "bring",
            stored,
            (whole, whole, rows_of(strip + 2 * D1, F32), jax.ShapeDtypeStruct((8, 128), F32)),
            (dma((3,)),),
            remote=range(3),
        )
        partner_far, feat_mid, mark = lax.optimization_barrier((partner_far, mid_given[1], mark))
        partner_mid = swap(feat_mid)
        (grad_far,) = call(
            grad_first,
            "grad_first",
            (*far_given, partner_far, vectors, mark),
            (rows_of(EDGE),),
            flops=0 * per_row,
        )
        far_grad = far(grad_far, inside)
        (grad_near,) = call(
            grad_first,
            "grad_near",
            (*near_given, partner_near, vectors, grad_far),
            (rows_of(EDGE),),
            flops=0 * per_row,
        )
        (grad_mid,) = call(
            gradient, "grad_mid", (*mid_given, partner_mid, vectors), (rows_of(mid),), flops=18 * per_row
        )
        (grads,) = call(
            gather, "gather", (far_grad, grad_far, grad_mid, grad_near, near(grad_near)), (rows_of(strip + 2 * EDGE),)
        )
        return grads, *brought

    if routed:
        moves = [
            functools.partial(lax.ppermute, axis_name=("peer", "space"), perm=spread(route, groups, space))
            for route in routes
        ]
        state = lax.switch(index[0], [functools.partial(exchange, move) for move in moves], *given, vectors, kernel2, kernel1, fold)
    else:
        state = exchange(functools.partial(swap_blocks, pairing=pairing), *given, vectors, kernel2, kernel1, fold)
    grads, kernel2, kernel1, fold = state
    back = strip + 2 * D1
    (out,) = call(
        backward,
        "backward",
        (grads, fold, kernel2, kernel1),
        (rows_of(strip),),
        (cat_of(strip + 2 * EDGE), cat_of(back), rows_of(back)),
        flops=per_row * (back + strip),
        result=0,
    )
    return out[None]


def solution(mesh):
    placed = (
        P("peer", "space", None, None),
        P("peer", "space", None, None),
        P(),
        P("peer", None, None, None, None),
        P("peer", None),
        P("peer", None),
        P("peer", None, None, None, None),
        P("peer", None),
        P("peer", None),
    )
    return jax.shard_map(
        per_device,
        mesh=mesh,
        in_specs=placed,
        out_specs=P("peer", "space", None, None),
        check_vma=False,
    )
```
